32 devices in a mesh: row: 4 (over y, core), col: 8 (over z, x).
Axes of the slice: x: 2, y: 2, z: 4, core: 2. Of those that a mesh axis runs over, the one named last changes fastest.
Arguments:
- scatter_vectors: float32 [2, 2, 3, 128, 4096], P(None, None, None, 'row', 'col'), may hold values from -80 to 80
- ground_ratio: float32 [3], replicated, may hold values from 0.1 to 1
- vertical_wavenumber: float32 [128, 4096], P('row', 'col'), may hold values from 0.45 to 1.1
- initial_phase: float32 [128, 4096], P('row', 'col'), may hold values from 0.1 to 3.6
- initial_extinction: float32 [128, 4096], P('row', 'col'), may hold values from 0.1 to 2.9
Outputs:
- heights: float32 [128, 4096], P('row', 'col')
- extinction_depth: float32 [128, 4096], P('row', 'col')
The draws below stay inside these ranges and needn't reach their ends.
All inputs are finite; a program needn't handle non-finite values.
Results may differ from the reference program's by a relative error of at most 0.00022.
Values sent between devices are 32-bit elements; how exact they have to be, the bound alone decides.
A program may use at most 64 MiB of HBM per device.

```python
import jax
import jax.numpy as jnp
from jax import lax

CHANNELS = 3
RADIUS = 9
LAYERS = 16
GAUSS_STEPS = 2
ITERS = 3
NY = 128
NX = 4096


def forest_scene(key):
    keys = jax.random.split(jax.random.fold_in(key, 4242), 8)
    ground = jnp.exp(jax.random.uniform(keys[0], (CHANNELS,), jnp.float32, jnp.log(0.1), jnp.log(1.0)))
    row_place = jnp.arange(NY, dtype=jnp.float32) / NY
    col_place = jnp.arange(NX, dtype=jnp.float32) / NX
    height_true = (1.2 + 1.2 * row_place)[:, None] * jax.random.uniform(keys[1], (NY, NX), jnp.float32, 0.8, 1.25)
    wavenumber = (0.5 + 0.5 * col_place)[None, :] * jax.random.uniform(keys[2], (NY, NX), jnp.float32, 0.9, 1.1)
    phase_true = height_true * wavenumber
    atten_true = jax.random.uniform(keys[3], (NY, NX), jnp.float32, 0.5, 2.5)
    weight_sum = jnp.zeros((NY, NX), jnp.float32)
    cosine_sum = jnp.zeros((NY, NX), jnp.float32)
    sine_sum = jnp.zeros((NY, NX), jnp.float32)
    for layer_index in range(LAYERS):
        layer_depth = (layer_index + 0.5) / LAYERS
        weight = jnp.exp(atten_true * layer_depth)
        weight_sum = weight_sum + weight
        cosine_sum = cosine_sum + weight * jnp.cos(phase_true * layer_depth)
        sine_sum = sine_sum + weight * jnp.sin(phase_true * layer_depth)
    volume_re = cosine_sum / weight_sum
    volume_im = sine_sum / weight_sum
    model_re = (volume_re[None] + ground[:, None, None]) / (1.0 + ground[:, None, None])
    model_im = volume_im[None] / (1.0 + ground[:, None, None])
    keep = jnp.sqrt(jnp.maximum(1.0 - model_re * model_re - model_im * model_im, 0.0))
    signal = jax.random.truncated_normal(keys[4], -4.0, 4.0, (2, CHANNELS, NY, NX), jnp.float32) * 0.7071
    noise = jax.random.truncated_normal(keys[5], -4.0, 4.0, (2, CHANNELS, NY, NX), jnp.float32) * 0.7071
    real_one = signal[0]
    imag_one = signal[1]
    real_two = model_re * real_one - model_im * imag_one + keep * noise[0]
    imag_two = model_re * imag_one + model_im * real_one + keep * noise[1]
    vectors = jnp.stack([jnp.stack([real_one, imag_one]), jnp.stack([real_two, imag_two])])
    phase_guess = phase_true + jax.random.uniform(keys[6], (NY, NX), jnp.float32, -0.25, 0.25)
    atten_guess = atten_true + jax.random.uniform(keys[7], (NY, NX), jnp.float32, -0.4, 0.4)
    return (vectors, ground, wavenumber, phase_guess, atten_guess)


def draw_scatter_vectors(key, part):
    return forest_scene(key)[0]


def draw_ground_ratio(key, part):
    return forest_scene(key)[1]


def draw_vertical_wavenumber(key, part):
    return forest_scene(key)[2]


def draw_initial_phase(key, part):
    return forest_scene(key)[3]


def draw_initial_extinction(key, part):
    return forest_scene(key)[4]


def setup_inputs(seed: int = 0) -> dict:
    splits = jax.random.split(jax.random.key(seed), 6)
    scatter_vectors = draw_scatter_vectors(jax.random.fold_in(splits[5], 71), 0)
    ground_ratio = draw_ground_ratio(jax.random.fold_in(splits[5], 71), 0)
    vertical_wavenumber = draw_vertical_wavenumber(jax.random.fold_in(splits[5], 71), 0)
    initial_phase = draw_initial_phase(jax.random.fold_in(splits[5], 71), 0)
    initial_extinction = draw_initial_extinction(jax.random.fold_in(splits[5], 71), 0)
    return {"scatter_vectors": scatter_vectors, "ground_ratio": ground_ratio, "vertical_wavenumber": vertical_wavenumber, "initial_phase": initial_phase, "initial_extinction": initial_extinction}


EPSILON = 1e-06
DAMPING = 0.002
SMOOTHING = 1.0

def product_fields(vectors):
    real_one = vectors[0, 0]
    imag_one = vectors[0, 1]
    real_two = vectors[1, 0]
    imag_two = vectors[1, 1]
    return jnp.stack([real_one * real_one + imag_one * imag_one, real_two * real_two + imag_two * imag_two, real_one * real_two + imag_one * imag_two, real_one * imag_two - imag_one * real_two])

def column_window(padded, radius):
    span_cols = padded.shape[-1] - 2 * radius
    running = padded[..., 0:span_cols]
    for offset in range(1, 2 * radius + 1):
        running = running + padded[..., offset:offset + span_cols]
    return running

def row_window(padded, radius):
    span_rows = padded.shape[-2] - 2 * radius
    running = padded[..., 0:span_rows, :]
    for offset in range(1, 2 * radius + 1):
        running = running + padded[..., offset:offset + span_rows, :]
    return running

def coherence_pair(window_sums):
    norm_scale = lax.rsqrt(window_sums[0] * window_sums[1] + EPSILON)
    return (window_sums[2] * norm_scale, window_sums[3] * norm_scale)

def channel_summary(coherence_re, coherence_im, ground_ratio):
    ground_weight = 1.0 / (1.0 + ground_ratio)
    weighted_re = lax.optimization_barrier(jnp.sum(coherence_re * ground_weight[:, None, None], axis=0))
    weighted_im = lax.optimization_barrier(jnp.sum(coherence_im * ground_weight[:, None, None], axis=0))
    weight_total = jnp.sum(ground_weight * ground_weight)
    offset_total = jnp.sum(ground_ratio * ground_weight * ground_weight)
    confidence = lax.optimization_barrier(jnp.mean(coherence_re * coherence_re + coherence_im * coherence_im, axis=0))
    return (weighted_re, weighted_im, weight_total, offset_total, confidence)

def volume_moments(phase_height, attenuation):
    weight_sum = jnp.zeros_like(phase_height)
    depth_sum = jnp.zeros_like(phase_height)
    cosine_sum = jnp.zeros_like(phase_height)
    sine_sum = jnp.zeros_like(phase_height)
    depth_cosine = jnp.zeros_like(phase_height)
    depth_sine = jnp.zeros_like(phase_height)
    for layer_index in range(LAYERS):
        layer_depth = (layer_index + 0.5) / LAYERS
        weight = jnp.exp(attenuation * layer_depth)
        cosine = weight * jnp.cos(phase_height * layer_depth)
        sine_term = weight * jnp.sin(phase_height * layer_depth)
        weight_sum = weight_sum + weight
        depth_sum = depth_sum + weight * layer_depth
        cosine_sum = cosine_sum + cosine
        sine_sum = sine_sum + sine_term
        depth_cosine = depth_cosine + cosine * layer_depth
        depth_sine = depth_sine + sine_term * layer_depth
    norm_scale = 1.0 / weight_sum
    return (depth_sum * norm_scale, cosine_sum * norm_scale, sine_sum * norm_scale, depth_cosine * norm_scale, depth_sine * norm_scale)

def gauss_newton(phase_height, attenuation, weighted_re, weighted_im, weight_total, offset_total):
    for gauss_step in range(GAUSS_STEPS):
        mean_depth, real_part, imag_part, depth_cosine, depth_sine = volume_moments(phase_height, attenuation)
        real_by_atten = depth_cosine - mean_depth * real_part
        real_by_phase = -depth_sine
        imag_by_atten = depth_sine - mean_depth * imag_part
        imag_by_phase = depth_cosine
        misfit_re = weighted_re - weight_total * real_part - offset_total
        misfit_im = weighted_im - weight_total * imag_part
        normal_aa = weight_total * (real_by_atten * real_by_atten + imag_by_atten * imag_by_atten) + DAMPING
        normal_ap = weight_total * (real_by_atten * real_by_phase + imag_by_atten * imag_by_phase)
        normal_pp = weight_total * (real_by_phase * real_by_phase + imag_by_phase * imag_by_phase) + DAMPING
        grad_atten = real_by_atten * misfit_re + imag_by_atten * misfit_im
        grad_phase = real_by_phase * misfit_re + imag_by_phase * misfit_im
        determinant = normal_aa * normal_pp - normal_ap * normal_ap
        new_atten = attenuation + (normal_pp * grad_atten - normal_ap * grad_phase) / determinant
        phase_height = phase_height + (normal_aa * grad_phase - normal_ap * grad_atten) / determinant
        attenuation = new_atten
    return (phase_height, attenuation)

def apply_operator(grid_field, confidence):
    padded = jnp.pad(grid_field, 1)
    beside = padded[2:, 1:-1] + padded[:-2, 1:-1] + padded[1:-1, 2:] + padded[1:-1, :-2]
    return confidence * grid_field + SMOOTHING * (4.0 * grid_field - beside)

def reference(scatter_vectors, ground_ratio, vertical_wavenumber, initial_phase, initial_extinction):
    real_parts = []
    imag_parts = []
    for channel in range(CHANNELS):
        fields = product_fields(scatter_vectors[:, :, channel:channel + 1])
        padded = jnp.pad(fields, ((0, 0), (0, 0), (RADIUS, RADIUS), (RADIUS, RADIUS)))
        window_sums = row_window(column_window(padded, RADIUS), RADIUS)
        coherence_re, coherence_im = coherence_pair(window_sums)
        real_parts.append(coherence_re)
        imag_parts.append(coherence_im)
    coherence_re = jnp.concatenate(real_parts, axis=0)
    coherence_im = jnp.concatenate(imag_parts, axis=0)
    weighted_re, weighted_im, weight_total, offset_total, confidence = channel_summary(coherence_re, coherence_im, ground_ratio)
    phase_height, extinction_depth = gauss_newton(initial_phase, initial_extinction, weighted_re, weighted_im, weight_total, offset_total)
    start_height = phase_height / vertical_wavenumber
    solution = start_height
    residual = confidence * start_height - apply_operator(start_height, confidence)
    direction = residual
    norm_now = jnp.sum(residual * residual)
    for iteration in range(ITERS):
        image_field = apply_operator(direction, confidence)
        step_length = norm_now / jnp.sum(direction * image_field)
        solution = solution + step_length * direction
        residual = residual - step_length * image_field
        norm_next = jnp.sum(residual * residual)
        direction = residual + norm_next / norm_now * direction
        norm_now = norm_next
    return (solution, extinction_depth)
```

```python
import functools

import jax
import jax.numpy as jnp
from jax import lax
from jax.experimental import pallas as pl
from jax.experimental.pallas import tpu as pltpu
from jax.sharding import PartitionSpec as P

RADIUS = 9
LAYERS = 16
GAUSS_STEPS = 2
ITERS = 3

EPSILON = 1e-06
DAMPING = 0.002
SMOOTHING = 1.0

CHANNELS = 3
RAW = 4 * CHANNELS
GUESS = 3
GHOST = ITERS + 1
REACH = RADIUS + GHOST
SLOT = 16
LANES = 128
SHIFT = 4.5 * SMOOTHING
MESH = pl.DeviceIdType.MESH


def turn(value, amount, axis):
    size = value.shape[axis]
    amount = amount % size
    return value if amount == 0 else pltpu.roll(value, amount, axis)


def window(value, axis):
    pair = value + turn(value, -1, axis)
    four = pair + turn(pair, -2, axis)
    eight = four + turn(four, -4, axis)
    most = eight + turn(eight, -8, axis)
    return most + turn(pair, -16, axis) + turn(value, -18, axis)


def sine_cosine(angle):
    square = angle * angle
    sine = -1.0 / 39916800.0 + square * (1.0 / 6227020800.0)
    for term in (362880.0, -5040.0, 120.0, -6.0):
        sine = sine * square + 1.0 / term
    sine = angle + angle * square * sine
    cosine = -1.0 / 3628800.0 + square * (1.0 / 479001600.0)
    for term in (40320.0, -720.0, 24.0, -2.0):
        cosine = cosine * square + 1.0 / term
    return sine, 1.0 + square * cosine


def volume_moments(phase, atten):
    sin_half, cos_half = sine_cosine(phase * (0.5 / LAYERS))
    sin_n = 2.0 * sin_half * cos_half
    cos_n = 1.0 - 2.0 * sin_half * sin_half
    grown = jnp.exp(atten * (1.0 / LAYERS))
    weight = 1.0 + grown
    depth = grown
    step_r = grown * cos_n
    step_i = grown * sin_n
    sum_r = 1.0 + step_r
    sum_i = step_i
    deep_r = step_r
    deep_i = step_i
    count = 2
    while count < LAYERS:
        sin_n, cos_n = 2.0 * sin_n * cos_n, 1.0 - 2.0 * sin_n * sin_n
        grown = jnp.exp(atten * (float(count) / LAYERS))
        step_r = grown * cos_n
        step_i = grown * sin_n
        depth = depth + grown * (depth + float(count) * weight)
        weight = weight + grown * weight
        inner_r = deep_r + float(count) * sum_r
        inner_i = deep_i + float(count) * sum_i
        deep_r = deep_r + (step_r * inner_r - step_i * inner_i)
        deep_i = deep_i + (step_r * inner_i + step_i * inner_r)
        sum_r, sum_i = (
            sum_r + (step_r * sum_r - step_i * sum_i),
            sum_i + (step_r * sum_i + step_i * sum_r),
        )
        count *= 2
    scale = 1.0 / weight
    fine = scale * (1.0 / LAYERS)
    deep_r = deep_r + 0.5 * sum_r
    deep_i = deep_i + 0.5 * sum_i
    return (
        depth * fine + 0.5 / LAYERS,
        (cos_half * sum_r - sin_half * sum_i) * scale,
        (cos_half * sum_i + sin_half * sum_r) * scale,
        (cos_half * deep_r - sin_half * deep_i) * fine,
        (cos_half * deep_i + sin_half * deep_r) * fine,
    )


def gauss_newton(phase, atten, weighted_re, weighted_im, weight_total, offset_total):
    for _ in range(GAUSS_STEPS):
        mean, real, imag, depth_cos, depth_sin = volume_moments(phase, atten)
        ra = depth_cos - mean * real
        rt = -depth_sin
        ia = depth_sin - mean * imag
        it = depth_cos
        er = weighted_re - weight_total * real - offset_total
        ei = weighted_im - weight_total * imag
        maa = weight_total * (ra * ra + ia * ia) + DAMPING
        map_ = weight_total * (ra * rt + ia * it)
        mpp = weight_total * (rt * rt + it * it) + DAMPING
        ga = ra * er + ia * ei
        gp = rt * er + it * ei
        over = 1.0 / (maa * mpp - map_ * map_)
        atten = atten + (mpp * ga - map_ * gp) * over
        phase = phase + (maa * gp - map_ * ga) * over
    return phase, atten


def dot_poly(left, right, moments):
    total = None
    for i, a in enumerate(left):
        for j, b in enumerate(right):
            term = a * b * moments[i + j]
            total = term if total is None else total + term
    return total


def add_poly(left, right, scale):
    size = max(len(left), len(right))
    out = []
    for i in range(size):
        if i >= len(right):
            out.append(left[i])
        elif i >= len(left):
            out.append(scale * right[i])
        else:
            out.append(left[i] + scale * right[i])
    return out


def solve_coefficients(moments):
    one = jnp.ones_like(moments[0])
    residual = [one]
    direction = [one]
    answer = []
    norm = moments[0]
    for iteration in range(ITERS):
        image = [SHIFT * d for d in direction] + [0.0 * one]
        for i, d in enumerate(direction):
            image[i + 1] = image[i + 1] + d
        step = norm / dot_poly(direction, image, moments)
        answer = add_poly(answer, direction, step)
        if iteration + 1 < ITERS:
            residual = add_poly(residual, image, -step)
            following = dot_poly(residual, residual, moments)
            direction = add_poly(residual, direction, following / norm)
            norm = following
    return answer


def kernel(
    counts, ratio, vectors, wavenumber, phase0, atten0, heights, extinction,
    row_send, row_recv, col_send, col_recv, corner_recv, fields, guess, sums,
    conf_buf, start_buf, mine, row_part, col_part,
    row_ss, row_rs, col_ss, col_rs, corner_ss, corner_rs, rsum_ss, rsum_rs, csum_ss, csum_rs,
):
    rows, cols = counts
    my_row = lax.axis_index("row")
    my_col = lax.axis_index("col")
    high, wide = phase0.shape
    full = wide + LANES
    tall = high + 2 * GHOST
    plain = (wavenumber, phase0, atten0)

    def row_peer(k):
        return lax.rem(my_row + k, rows)

    def col_peer(k):
        return lax.rem(my_col + k, cols)

    barrier = pltpu.get_barrier_semaphore()
    for k in range(1, rows):
        pl.semaphore_signal(barrier, inc=1, device_id=(row_peer(k), my_col), device_id_type=MESH)
    for k in range(1, cols):
        pl.semaphore_signal(barrier, inc=1, device_id=(my_row, col_peer(k)), device_id_type=MESH)

    has = (my_row > 0, my_row < rows - 1)
    beside = (my_col > 0, my_col < cols - 1)

    for f in range(RAW):
        row_send[0, f * REACH : (f + 1) * REACH, :] = vectors[f, 0:REACH, :]
        row_send[1, f * REACH : (f + 1) * REACH, :] = vectors[f, high - REACH : high, :]
    base = RAW * REACH
    for g in range(GUESS):
        row_send[0, base + g * GHOST : base + (g + 1) * GHOST, :] = plain[g][0:GHOST, :]
        row_send[1, base + g * GHOST : base + (g + 1) * GHOST, :] = plain[g][high - GHOST : high, :]

    lane = lax.broadcasted_iota(jnp.int32, (high, LANES), 1)
    per = LANES // SLOT
    packs = (RAW + GUESS + per - 1) // per
    for k in range(packs):
        low = jnp.zeros((high, LANES), jnp.float32)
        top = jnp.zeros((high, LANES), jnp.float32)
        for p in range(per):
            f = k * per + p
            if f >= RAW + GUESS:
                continue
            if f < RAW:
                first, last = vectors[f, :, 0:LANES], vectors[f, :, wide - LANES : wide]
            else:
                ref = plain[f - RAW]
                first, last = ref[:, 0:LANES], ref[:, wide - LANES : wide]
            here = (lane >= p * SLOT) & (lane < (p + 1) * SLOT)
            low = jnp.where(here, turn(first, p * SLOT, 1), low)
            top = jnp.where(here, turn(last, (p + 1) * SLOT, 1), top)
        col_send[0, :, k * LANES : (k + 1) * LANES] = low
        col_send[1, :, k * LANES : (k + 1) * LANES] = top

    pl.semaphore_wait(barrier, rows + cols - 2)

    def row_copy(side):
        return pltpu.make_async_remote_copy(
            src_ref=row_send.at[side],
            dst_ref=row_recv.at[1 - side],
            send_sem=row_ss.at[side],
            recv_sem=row_rs.at[1 - side],
            device_id=(my_row - 1 + 2 * side, my_col),
            device_id_type=MESH,
        )

    def col_copy(side):
        return pltpu.make_async_remote_copy(
            src_ref=col_send.at[side],
            dst_ref=col_recv.at[1 - side],
            send_sem=col_ss.at[side],
            recv_sem=col_rs.at[1 - side],
            device_id=(my_row, my_col - 1 + 2 * side),
            device_id_type=MESH,
        )

    def corner_copy(side):
        begin = 0 if side == 0 else high - SLOT
        return pltpu.make_async_remote_copy(
            src_ref=col_recv.at[:, begin : begin + SLOT, :],
            dst_ref=corner_recv.at[1 - side],
            send_sem=corner_ss.at[side],
            recv_sem=corner_rs.at[1 - side],
            device_id=(my_row - 1 + 2 * side, my_col),
            device_id_type=MESH,
        )

    for side in (0, 1):
        pl.when(has[side])(lambda side=side: row_copy(side).start())
    for side in (0, 1):
        pl.when(beside[side])(lambda side=side: col_copy(side).start())

    for side in (0, 1):
        @pl.when(jnp.logical_not(has[side]))
        def _(side=side):
            row_recv[side] = jnp.zeros(row_recv.shape[1:], jnp.float32)
            corner_recv[side] = jnp.zeros(corner_recv.shape[1:], jnp.float32)

        @pl.when(jnp.logical_not(beside[side]))
        def _(side=side):
            col_recv[side] = jnp.zeros(col_recv.shape[1:], jnp.float32)

    for f in range(RAW):
        fields[f, REACH : REACH + high, 0:wide] = vectors[f]
    for g in range(GUESS):
        guess[g, GHOST : GHOST + high, 0:wide] = plain[g][...]

    for side in (0, 1):
        pl.when(beside[side])(lambda side=side: col_copy(1 - side).wait_recv())
    for side in (0, 1):
        pl.when(has[side])(lambda side=side: corner_copy(side).start())

    def unpacked(left, right, f):
        p = f % per
        place = lax.broadcasted_iota(jnp.int32, left.shape, 1)
        return jnp.where(
            place < LANES // 2,
            turn(right, -p * SLOT, 1),
            turn(left, LANES - SLOT - p * SLOT, 1),
        )

    for f in range(RAW + GUESS):
        k = f // per
        piece = slice(k * LANES, (k + 1) * LANES)
        value = unpacked(col_recv[0, :, piece], col_recv[1, :, piece], f)
        if f < RAW:
            fields[f, REACH : REACH + high, wide:full] = value
        else:
            guess[f - RAW, GHOST : GHOST + high, wide:full] = value

    for side in (0, 1):
        @pl.when(has[side])
        def _(side=side):
            row_copy(1 - side).wait_recv()
            corner_copy(1 - side).wait_recv()

    filled = 2 * REACH + high
    for f in range(RAW + GUESS):
        k = f // per
        piece = slice(k * LANES, (k + 1) * LANES)
        above = unpacked(corner_recv[0, 0, :, piece], corner_recv[0, 1, :, piece], f)
        below = unpacked(corner_recv[1, 0, :, piece], corner_recv[1, 1, :, piece], f)
        if f < RAW:
            fields[f, 0:REACH, 0:wide] = row_recv[0, f * REACH : (f + 1) * REACH, :]
            fields[f, REACH + high : filled, 0:wide] = row_recv[1, f * REACH : (f + 1) * REACH, :]
            fields[f, 0:REACH, wide:full] = above[SLOT - REACH :, :]
            fields[f, REACH + high : filled, wide:full] = below[0:REACH, :]
            fields[f, filled:, :] = jnp.zeros((fields.shape[1] - filled, full), jnp.float32)
        else:
            g = f - RAW
            span = slice(base + g * GHOST, base + (g + 1) * GHOST)
            guess[g, 0:GHOST, 0:wide] = row_recv[0, span, :]
            guess[g, GHOST + high : tall, 0:wide] = row_recv[1, span, :]
            guess[g, 0:GHOST, wide:full] = above[SLOT - GHOST :, :]
            guess[g, GHOST + high : tall, wide:full] = below[0:GHOST, :]

    def row_sums(channel, carry):
        for strip in range(full // LANES):
            piece = slice(strip * LANES, (strip + 1) * LANES)
            re1 = fields[channel, :, piece]
            im1 = fields[CHANNELS + channel, :, piece]
            re2 = fields[2 * CHANNELS + channel, :, piece]
            im2 = fields[3 * CHANNELS + channel, :, piece]
            products = (
                re1 * re1 + im1 * im1,
                re2 * re2 + im2 * im2,
                re1 * re2 + im1 * im2,
                re1 * im2 - im1 * re2,
            )
            for i, product in enumerate(products):
                sums[4 * channel + i, :, piece] = window(product, 0)[0:tall, :]
        return carry

    lax.fori_loop(0, CHANNELS, row_sums, 0)

    ratios = [jnp.full((1, full), ratio[k], jnp.float32) for k in range(CHANNELS)]
    weights = [1.0 / (1.0 + r) for r in ratios]
    weight_total = sum(w * w for w in weights)
    offset_total = sum(r * w * w for r, w in zip(ratios, weights))

    def fit(chunk, carry):
        at = pl.multiple_of(chunk * 8, 8)
        block = pl.ds(at, 8)
        weighted_re = weighted_im = confidence = None
        for k in range(CHANNELS):
            power1, power2, cross_re, cross_im = [
                turn(window(sums[4 * k + i, block, :], 1), RADIUS, 1) for i in range(4)
            ]
            scale = lax.rsqrt(power1 * power2 + EPSILON)
            real = cross_re * scale
            imag = cross_im * scale
            parts = (real * weights[k], imag * weights[k], real * real + imag * imag)
            if k == 0:
                weighted_re, weighted_im, confidence = parts
            else:
                weighted_re = weighted_re + parts[0]
                weighted_im = weighted_im + parts[1]
                confidence = confidence + parts[2]
        phase, atten = gauss_newton(
            guess[1, block, :], guess[2, block, :], weighted_re, weighted_im,
            weight_total, offset_total,
        )
        conf_buf[block, :] = confidence * (1.0 / CHANNELS)
        start_buf[0, block, :] = phase / guess[0, block, :]
        start_buf[1, block, :] = atten
        return carry

    lax.fori_loop(0, tall // 8, fit, 0)

    row_at = lax.broadcasted_iota(jnp.int32, (tall, full), 0) - GHOST
    lane_at = lax.broadcasted_iota(jnp.int32, (tall, full), 1)
    col_at = jnp.where(lane_at < wide + LANES // 2, lane_at, lane_at - full)
    near = (col_at >= -GHOST) & (col_at < wide + GHOST)
    row_all = row_at + my_row * high
    col_all = col_at + my_col * wide
    inside = near & (row_all >= 0) & (row_all < rows * high) & (col_all >= 0) & (col_all < cols * wide)

    def masked(value):
        return jnp.where(inside, value, 0.0)

    def around(value):
        return turn(value, 1, 0) + turn(value, -1, 0) + turn(value, 1, 1) + turn(value, -1, 1)

    start = masked(start_buf[0])
    confidence = conf_buf[...]
    centred = confidence + (4.0 * SMOOTHING - SHIFT)
    basis = [masked(SMOOTHING * (around(start) - 4.0 * start))]
    for _ in range(ITERS - 1):
        basis.append(masked(centred * basis[-1] - SMOOTHING * around(basis[-1])))
    basis.append(centred * basis[-1] - SMOOTHING * around(basis[-1]))

    extinction[...] = start_buf[1, GHOST : GHOST + high, 0:wide]
    own = inside & (row_at >= 0) & (row_at < high) & (lane_at < wide)
    for m in range(2 * ITERS):
        product = jnp.where(own, basis[m // 2] * basis[m - m // 2], 0.0)
        line = jnp.sum(product, axis=0, keepdims=True)
        total = line[:, 0:LANES]
        for strip in range(1, wide // LANES):
            total = total + line[:, strip * LANES : (strip + 1) * LANES]
        mine[m : m + 1, :] = total
    mine[2 * ITERS :, :] = jnp.zeros((8 - 2 * ITERS, LANES), jnp.float32)
    start_buf[0] = start
    for i in range(ITERS):
        fields[i, 0:tall, :] = basis[i]

    def row_share(k):
        return pltpu.make_async_remote_copy(
            src_ref=mine,
            dst_ref=row_part.at[my_row],
            send_sem=rsum_ss.at[k],
            recv_sem=rsum_rs.at[my_row],
            device_id=(row_peer(k), my_col),
            device_id_type=MESH,
        )

    def row_arrival(k):
        who = row_peer(k)
        return pltpu.make_async_remote_copy(
            src_ref=mine,
            dst_ref=row_part.at[who],
            send_sem=rsum_ss.at[k],
            recv_sem=rsum_rs.at[who],
            device_id=(who, my_col),
            device_id_type=MESH,
        )

    for k in range(1, rows):
        row_share(k).start()
    row_part[my_row] = mine[...]
    for k in range(1, rows):
        row_arrival(k).wait_recv()
    strip_sum = row_part[0]
    for k in range(1, rows):
        strip_sum = strip_sum + row_part[k]
    col_part[my_col] = strip_sum

    def col_share(k, slot):
        return pltpu.make_async_remote_copy(
            src_ref=col_part.at[my_col],
            dst_ref=col_part.at[slot],
            send_sem=csum_ss.at[k],
            recv_sem=csum_rs.at[slot],
            device_id=(my_row, col_peer(k)),
            device_id_type=MESH,
        )

    for k in range(1, cols):
        col_share(k, my_col).start()
    for k in range(1, cols):
        col_share(k, col_peer(k)).wait_recv()
    everything = col_part[0]
    for k in range(1, cols):
        everything = everything + col_part[k]
    everything = jnp.sum(everything, axis=1, keepdims=True)
    moments = [everything[m : m + 1, :] for m in range(2 * ITERS)]
    answer = solve_coefficients(moments)
    result = start_buf[0, GHOST : GHOST + high, 0:wide]
    for i, scale in enumerate(answer):
        result = result + scale * fields[i, GHOST : GHOST + high, 0:wide]
    heights[...] = result

    for side in (0, 1):
        @pl.when(has[side])
        def _(side=side):
            row_copy(side).wait_send()
            corner_copy(side).wait_send()

        pl.when(beside[side])(lambda side=side: col_copy(side).wait_send())
    for k in range(1, rows):
        row_share(k).wait_send()
    for k in range(1, cols):
        col_share(k, my_col).wait_send()


def local(counts, scatter_vectors, ground_ratio, vertical_wavenumber, initial_phase, initial_extinction):
    high, wide = initial_phase.shape
    rows, cols = counts
    vectors = scatter_vectors.reshape(RAW, high, wide)
    full = wide + LANES
    tall = high + 2 * GHOST
    deep = -(-(2 * REACH + high) // 8) * 8
    edge = -(-(RAW * REACH + GUESS * GHOST) // 8) * 8
    packed = -(-(RAW + GUESS) * SLOT // LANES) * LANES
    vmem = pl.BlockSpec(memory_space=pltpu.VMEM)
    f32 = jnp.float32
    dma = pltpu.SemaphoreType.DMA
    out = jax.ShapeDtypeStruct((high, wide), f32)
    heights, extinction = pl.pallas_call(
        functools.partial(kernel, counts),
        out_shape=(out, out),
        in_specs=[pl.BlockSpec(memory_space=pltpu.SMEM)] + [vmem] * 4,
        out_specs=(vmem, vmem),
        scratch_shapes=[
            pltpu.VMEM((2, edge, wide), f32),
            pltpu.VMEM((2, edge, wide), f32),
            pltpu.VMEM((2, high, packed), f32),
            pltpu.VMEM((2, high, packed), f32),
            pltpu.VMEM((2, 2, SLOT, packed), f32),
            pltpu.VMEM((RAW, deep, full), f32),
            pltpu.VMEM((GUESS, tall, full), f32),
            pltpu.VMEM((RAW, tall, full), f32),
            pltpu.VMEM((tall, full), f32),
            pltpu.VMEM((2, tall, full), f32),
            pltpu.VMEM((8, LANES), f32),
            pltpu.VMEM((rows, 8, LANES), f32),
            pltpu.VMEM((cols, 8, LANES), f32),
            dma((2,)), dma((2,)), dma((2,)), dma((2,)), dma((2,)), dma((2,)),
            dma((rows,)), dma((rows,)), dma((cols,)), dma((cols,)),
        ],
        compiler_params=pltpu.CompilerParams(
            collective_id=0, has_side_effects=True, vmem_limit_bytes=32 * 1024 * 1024
        ),
        cost_estimate=pl.CostEstimate(
            flops=2000 * high * wide, bytes_accessed=80 * high * wide, transcendentals=8 * high * wide
        ),
    )(ground_ratio, vectors, vertical_wavenumber, initial_phase, initial_extinction)
    return (heights, extinction)


def solution(mesh):
    placed = (
        P(None, None, None, "row", "col"),
        P(),
        P("row", "col"),
        P("row", "col"),
        P("row", "col"),
    )
    counts = (mesh.shape["row"], mesh.shape["col"])
    return jax.shard_map(
        functools.partial(local, counts),
        mesh=mesh,
        in_specs=placed,
        out_specs=(P("row", "col"), P("row", "col")),
        check_vma=False,
    )
```

```python
import functools

import jax
import jax.numpy as jnp
from jax import lax
from jax.experimental import pallas as pl
from jax.experimental.pallas import tpu as pltpu
from jax.sharding import PartitionSpec as P

RADIUS = 9
LAYERS = 16
GAUSS_STEPS = 2
ITERS = 3

EPSILON = 1e-06
DAMPING = 0.002
SMOOTHING = 1.0

CHANNELS = 3
RAW = 4 * CHANNELS
GUESS = 3
GHOST = ITERS + 1
REACH = RADIUS + GHOST
SLOT = 16
LANES = 128
SHIFT = 4.5 * SMOOTHING
MESH = pl.DeviceIdType.MESH


def turn(value, amount, axis):
    size = value.shape[axis]
    amount = amount % size
    return value if amount == 0 else pltpu.roll(value, amount, axis)


def window(value, axis):
    pair = value + turn(value, -1, axis)
    four = pair + turn(pair, -2, axis)
    eight = four + turn(four, -4, axis)
    most = eight + turn(eight, -8, axis)
    return most + turn(pair, -16, axis) + turn(value, -18, axis)


def sine_cosine(angle):
    square = angle * angle
    sine = -1.0 / 39916800.0 + square * (1.0 / 6227020800.0)
    for term in (362880.0, -5040.0, 120.0, -6.0):
        sine = sine * square + 1.0 / term
    sine = angle + angle * square * sine
    cosine = -1.0 / 3628800.0 + square * (1.0 / 479001600.0)
    for term in (40320.0, -720.0, 24.0, -2.0):
        cosine = cosine * square + 1.0 / term
    return sine, 1.0 + square * cosine


def volume_moments(phase, atten):
    sin_half, cos_half = sine_cosine(phase * (0.5 / LAYERS))
    sin_n = 2.0 * sin_half * cos_half
    cos_n = 1.0 - 2.0 * sin_half * sin_half
    grown = jnp.exp(atten * (1.0 / LAYERS))
    weight = 1.0 + grown
    depth = grown
    step_r = grown * cos_n
    step_i = grown * sin_n
    sum_r = 1.0 + step_r
    sum_i = step_i
    deep_r = step_r
    deep_i = step_i
    count = 2
    while count < LAYERS:
        sin_n, cos_n = 2.0 * sin_n * cos_n, 1.0 - 2.0 * sin_n * sin_n
        grown = jnp.exp(atten * (float(count) / LAYERS))
        step_r = grown * cos_n
        step_i = grown * sin_n
        depth = depth + grown * (depth + float(count) * weight)
        weight = weight + grown * weight
        inner_r = deep_r + float(count) * sum_r
        inner_i = deep_i + float(count) * sum_i
        deep_r = deep_r + (step_r * inner_r - step_i * inner_i)
        deep_i = deep_i + (step_r * inner_i + step_i * inner_r)
        sum_r, sum_i = (
            sum_r + (step_r * sum_r - step_i * sum_i),
            sum_i + (step_r * sum_i + step_i * sum_r),
        )
        count *= 2
    scale = 1.0 / weight
    fine = scale * (1.0 / LAYERS)
    deep_r = deep_r + 0.5 * sum_r
    deep_i = deep_i + 0.5 * sum_i
    return (
        depth * fine + 0.5 / LAYERS,
        (cos_half * sum_r - sin_half * sum_i) * scale,
        (cos_half * sum_i + sin_half * sum_r) * scale,
        (cos_half * deep_r - sin_half * deep_i) * fine,
        (cos_half * deep_i + sin_half * deep_r) * fine,
    )


def gauss_newton(phase, atten, weighted_re, weighted_im, weight_total, offset_total):
    for _ in range(GAUSS_STEPS):
        mean, real, imag, depth_cos, depth_sin = volume_moments(phase, atten)
        ra = depth_cos - mean * real
        rt = -depth_sin
        ia = depth_sin - mean * imag
        it = depth_cos
        er = weighted_re - weight_total * real - offset_total
        ei = weighted_im - weight_total * imag
        maa = weight_total * (ra * ra + ia * ia) + DAMPING
        map_ = weight_total * (ra * rt + ia * it)
        mpp = weight_total * (rt * rt + it * it) + DAMPING
        ga = ra * er + ia * ei
        gp = rt * er + it * ei
        over = 1.0 / (maa * mpp - map_ * map_)
        atten = atten + (mpp * ga - map_ * gp) * over
        phase = phase + (maa * gp - map_ * ga) * over
    return phase, atten


def dot_poly(left, right, moments):
    total = None
    for i, a in enumerate(left):
        for j, b in enumerate(right):
            term = a * b * moments[i + j]
            total = term if total is None else total + term
    return total


def add_poly(left, right, scale):
    size = max(len(left), len(right))
    out = []
    for i in range(size):
        if i >= len(right):
            out.append(left[i])
        elif i >= len(left):
            out.append(scale * right[i])
        else:
            out.append(left[i] + scale * right[i])
    return out


def solve_coefficients(moments):
    one = jnp.ones_like(moments[0])
    residual = [one]
    direction = [one]
    answer = []
    norm = moments[0]
    for iteration in range(ITERS):
        image = [SHIFT * d for d in direction] + [0.0 * one]
        for i, d in enumerate(direction):
            image[i + 1] = image[i + 1] + d
        step = norm / dot_poly(direction, image, moments)
        answer = add_poly(answer, direction, step)
        if iteration + 1 < ITERS:
            residual = add_poly(residual, image, -step)
            following = dot_poly(residual, residual, moments)
            direction = add_poly(residual, direction, following / norm)
            norm = following
    return answer


def kernel(
    counts, ratio_in, vectors_in, wavenumber_in, phase_in, atten_in, heights, extinction,
    ratio, vectors, wavenumber, phase0, atten0, load_sem, row_send, row_recv, col_send, col_recv, corner_recv, fields, guess, sums,
    conf_buf, start_buf, mine, row_part, col_part,
    row_ss, row_rs, col_ss, col_rs, corner_ss, corner_rs, rsum_ss, rsum_rs, csum_ss, csum_rs,
):
    rows, cols = counts
    my_row = lax.axis_index("row")
    my_col = lax.axis_index("col")
    high, wide = phase0.shape
    full = wide + LANES
    tall = high + 2 * GHOST
    plain = (wavenumber, phase0, atten0)

    loads = [
        pltpu.make_async_copy(source, target, load_sem.at[i])
        for i, (source, target) in enumerate((
            (vectors_in, vectors), (wavenumber_in, wavenumber),
            (phase_in, phase0), (atten_in, atten0), (ratio_in, ratio),
        ))
    ]
    for load in loads:
        load.start()

    def row_peer(k):
        return lax.rem(my_row + k, rows)

    def col_peer(k):
        return lax.rem(my_col + k, cols)

    barrier = pltpu.get_barrier_semaphore()
    for k in range(1, rows):
        pl.semaphore_signal(barrier, inc=1, device_id=(row_peer(k), my_col), device_id_type=MESH)
    for k in range(1, cols):
        pl.semaphore_signal(barrier, inc=1, device_id=(my_row, col_peer(k)), device_id_type=MESH)

    has = (my_row > 0, my_row < rows - 1)
    beside = (my_col > 0, my_col < cols - 1)

    sent = row_send.shape[1]
    for side in (0, 1):
        row_recv[side, sent:, :] = jnp.zeros((row_recv.shape[1] - sent, wide), jnp.float32)
    first_row = GUESS * GHOST
    for load in loads:
        load.wait()
    for g in range(GUESS):
        row_send[0, g * GHOST : (g + 1) * GHOST, :] = plain[g][0:GHOST, :]
        row_send[1, g * GHOST : (g + 1) * GHOST, :] = plain[g][high - GHOST : high, :]
    for f in range(RAW):
        span = slice(first_row + f * REACH, first_row + (f + 1) * REACH)
        row_send[0, span, :] = vectors[f, 0:REACH, :]
        row_send[1, span, :] = vectors[f, high - REACH : high, :]

    def row_copy(side):
        return pltpu.make_async_remote_copy(
            src_ref=row_send.at[side],
            dst_ref=row_recv.at[1 - side, 0:sent, :],
            send_sem=row_ss.at[side],
            recv_sem=row_rs.at[1 - side],
            device_id=(my_row - 1 + 2 * side, my_col),
            device_id_type=MESH,
        )

    def col_copy(side):
        return pltpu.make_async_remote_copy(
            src_ref=col_send.at[side],
            dst_ref=col_recv.at[1 - side],
            send_sem=col_ss.at[side],
            recv_sem=col_rs.at[1 - side],
            device_id=(my_row, my_col - 1 + 2 * side),
            device_id_type=MESH,
        )

    def corner_copy(side):
        begin = 0 if side == 0 else high - SLOT
        return pltpu.make_async_remote_copy(
            src_ref=col_recv.at[:, begin : begin + SLOT, :],
            dst_ref=corner_recv.at[1 - side],
            send_sem=corner_ss.at[side],
            recv_sem=corner_rs.at[1 - side],
            device_id=(my_row - 1 + 2 * side, my_col),
            device_id_type=MESH,
        )

    pl.semaphore_wait(barrier, rows + cols - 2)
    for side in (0, 1):
        pl.when(has[side])(lambda side=side: row_copy(side).start())

    lane = lax.broadcasted_iota(jnp.int32, (high, LANES), 1)
    per = LANES // SLOT
    packs = (RAW + GUESS + per - 1) // per
    for k in range(packs):
        low = jnp.zeros((high, LANES), jnp.float32)
        top = jnp.zeros((high, LANES), jnp.float32)
        for p in range(per):
            f = k * per + p
            if f >= RAW + GUESS:
                continue
            if f < RAW:
                first, last = vectors[f, :, 0:LANES], vectors[f, :, wide - LANES : wide]
            else:
                ref = plain[f - RAW]
                first, last = ref[:, 0:LANES], ref[:, wide - LANES : wide]
            here = (lane >= p * SLOT) & (lane < (p + 1) * SLOT)
            low = jnp.where(here, turn(first, p * SLOT, 1), low)
            top = jnp.where(here, turn(last, (p + 1) * SLOT, 1), top)
        col_send[0, :, k * LANES : (k + 1) * LANES] = low
        col_send[1, :, k * LANES : (k + 1) * LANES] = top

    for side in (0, 1):
        pl.when(beside[side])(lambda side=side: col_copy(side).start())

    for side in (0, 1):
        @pl.when(jnp.logical_not(has[side]))
        def _(side=side):
            row_recv[side] = jnp.zeros(row_recv.shape[1:], jnp.float32)
            corner_recv[side] = jnp.zeros(corner_recv.shape[1:], jnp.float32)

        @pl.when(jnp.logical_not(beside[side]))
        def _(side=side):
            col_recv[side] = jnp.zeros(col_recv.shape[1:], jnp.float32)

    def products(raws):
        re1, im1, re2, im2 = raws
        return (
            re1 * re1 + im1 * im1,
            re2 * re2 + im2 * im2,
            re1 * re2 + im1 * im2,
            re1 * im2 - im1 * re2,
        )

    deep = -(-(2 * REACH + high) // 8) * 8
    above_own = jnp.zeros((REACH, LANES), jnp.float32)
    below_own = jnp.zeros((deep - REACH - high, LANES), jnp.float32)

    def own_sums(channel, raws, piece):
        for i, product in enumerate(products(raws)):
            placed = jnp.concatenate([above_own, product, below_own], axis=0)
            sums[4 * channel + i, :, piece] = window(placed, 0)[0:tall, :]

    def inner_sums(channel, carry):
        for strip in range(wide // LANES):
            piece = slice(strip * LANES, (strip + 1) * LANES)
            own_sums(channel, [vectors[CHANNELS * i + channel, :, piece] for i in range(4)], piece)
        return carry

    lax.fori_loop(0, CHANNELS, inner_sums, 0)
    for g in range(GUESS):
        guess[g, GHOST : GHOST + high, 0:wide] = plain[g][...]

    for side in (0, 1):
        pl.when(beside[side])(lambda side=side: col_copy(1 - side).wait_recv())
    for side in (0, 1):
        pl.when(has[side])(lambda side=side: corner_copy(side).start())

    def unpacked(left, right, f):
        p = f % per
        place = lax.broadcasted_iota(jnp.int32, left.shape, 1)
        return jnp.where(
            place < LANES // 2,
            turn(right, -p * SLOT, 1),
            turn(left, LANES - SLOT - p * SLOT, 1),
        )

    def outer(f):
        piece = slice(f // per * LANES, (f // per + 1) * LANES)
        return unpacked(col_recv[0, :, piece], col_recv[1, :, piece], f)

    for channel in range(CHANNELS):
        own_sums(channel, [outer(CHANNELS * i + channel) for i in range(4)], slice(wide, full))
    for g in range(GUESS):
        guess[g, GHOST : GHOST + high, wide:full] = outer(RAW + g)

    ratios = [jnp.full((1, full), ratio[k], jnp.float32) for k in range(CHANNELS)]
    weights = [1.0 / (1.0 + r) for r in ratios]
    weight_total = sum(w * w for w in weights)
    offset_total = sum(r * w * w for r, w in zip(ratios, weights))

    def fit(chunk):
        block = pl.ds(pl.multiple_of(chunk * 8, 8), 8)
        found = None
        for k in range(CHANNELS):
            power1, power2, cross_re, cross_im = [
                window(sums[4 * k + i, block, :], 1) for i in range(4)
            ]
            scale = lax.rsqrt(power1 * power2 + EPSILON)
            real = cross_re * scale
            imag = cross_im * scale
            parts = (real * weights[k], imag * weights[k], real * real + imag * imag)
            found = parts if k == 0 else [a + b for a, b in zip(found, parts)]
        weighted_re, weighted_im, confidence = [turn(a, RADIUS, 1) for a in found]
        phase, atten = gauss_newton(
            guess[1, block, :], guess[2, block, :], weighted_re, weighted_im,
            weight_total, offset_total,
        )
        conf_buf[block, :] = confidence * (1.0 / CHANNELS)
        start_buf[0, block, :] = phase / guess[0, block, :]
        start_buf[1, block, :] = atten

    chunks = tall // 8
    edge_chunks = SLOT // 8

    def middle(chunk, carry):
        fit(chunk)
        return carry

    lax.fori_loop(edge_chunks, chunks - edge_chunks, middle, 0)

    for side in (0, 1):
        @pl.when(has[side])
        def _(side=side):
            row_copy(1 - side).wait_recv()
            corner_copy(1 - side).wait_recv()

    line = lax.broadcasted_iota(jnp.int32, (SLOT, LANES), 0)
    keep = (line < REACH, line >= SLOT - REACH)

    def running(value, down):
        for k in (1, 2, 4, 8):
            if down:
                value = value + jnp.where(line >= k, turn(value, k, 0), 0.0)
            else:
                value = value + jnp.where(line < SLOT - k, turn(value, -k, 0), 0.0)
        return value

    def corner(side, f):
        piece = slice(f // per * LANES, (f // per + 1) * LANES)
        return unpacked(corner_recv[side, 0, :, piece], corner_recv[side, 1, :, piece], f)

    def halo_rows(side, f, strip):
        if strip < wide // LANES:
            begin = first_row + f * REACH - side * (SLOT - REACH)
            value = row_recv[side, begin : begin + SLOT, strip * LANES : (strip + 1) * LANES]
        else:
            value = turn(corner(side, f), (1 - 2 * side) * (REACH - SLOT), 0)
        return jnp.where(keep[side], value, 0.0)

    for side in (0, 1):
        begin = side * (tall - SLOT)
        for channel in range(CHANNELS):
            for strip in range(full // LANES):
                piece = slice(strip * LANES, (strip + 1) * LANES)
                raws = [halo_rows(side, CHANNELS * i + channel, strip) for i in range(4)]
                for i, product in enumerate(products(raws)):
                    sums[4 * channel + i, begin : begin + SLOT, piece] += running(product, side == 1)
    for g in range(GUESS):
        span = slice(g * GHOST, (g + 1) * GHOST)
        guess[g, 0:GHOST, 0:wide] = row_recv[0, span, :]
        guess[g, GHOST + high : tall, 0:wide] = row_recv[1, span, :]
        guess[g, 0:GHOST, wide:full] = corner(0, RAW + g)[SLOT - GHOST :, :]
        guess[g, GHOST + high : tall, wide:full] = corner(1, RAW + g)[0:GHOST, :]

    def edges(step, carry):
        fit(step + step // edge_chunks * (chunks - 2 * edge_chunks))
        return carry

    lax.fori_loop(0, 2 * edge_chunks, edges, 0)

    row_at = lax.broadcasted_iota(jnp.int32, (tall, full), 0) - GHOST
    lane_at = lax.broadcasted_iota(jnp.int32, (tall, full), 1)
    col_at = jnp.where(lane_at < wide + LANES // 2, lane_at, lane_at - full)
    near = (col_at >= -GHOST) & (col_at < wide + GHOST)
    row_all = row_at + my_row * high
    col_all = col_at + my_col * wide
    inside = near & (row_all >= 0) & (row_all < rows * high) & (col_all >= 0) & (col_all < cols * wide)

    def masked(value):
        return jnp.where(inside, value, 0.0)

    def around(value):
        return turn(value, 1, 0) + turn(value, -1, 0) + turn(value, 1, 1) + turn(value, -1, 1)

    start = masked(start_buf[0])
    confidence = conf_buf[...]
    centred = confidence + (4.0 * SMOOTHING - SHIFT)
    basis = [masked(SMOOTHING * (around(start) - 4.0 * start))]
    for _ in range(ITERS - 1):
        basis.append(masked(centred * basis[-1] - SMOOTHING * around(basis[-1])))
    basis.append(centred * basis[-1] - SMOOTHING * around(basis[-1]))

    extinction[...] = start_buf[1, GHOST : GHOST + high, 0:wide]
    own = inside & (row_at >= 0) & (row_at < high) & (lane_at < wide)
    for m in range(2 * ITERS):
        product = jnp.where(own, basis[m // 2] * basis[m - m // 2], 0.0)
        line = jnp.sum(product, axis=0, keepdims=True)
        total = line[:, 0:LANES]
        for strip in range(1, wide // LANES):
            total = total + line[:, strip * LANES : (strip + 1) * LANES]
        mine[m : m + 1, :] = total
    mine[2 * ITERS :, :] = jnp.zeros((8 - 2 * ITERS, LANES), jnp.float32)
    start_buf[0] = start
    for i in range(ITERS):
        fields[i] = basis[i]

    def row_share(k):
        return pltpu.make_async_remote_copy(
            src_ref=mine,
            dst_ref=row_part.at[my_row],
            send_sem=rsum_ss.at[k],
            recv_sem=rsum_rs.at[my_row],
            device_id=(row_peer(k), my_col),
            device_id_type=MESH,
        )

    def row_arrival(k):
        who = row_peer(k)
        return pltpu.make_async_remote_copy(
            src_ref=mine,
            dst_ref=row_part.at[who],
            send_sem=rsum_ss.at[k],
            recv_sem=rsum_rs.at[who],
            device_id=(who, my_col),
            device_id_type=MESH,
        )

    for k in range(1, rows):
        row_share(k).start()
    row_part[my_row] = mine[...]
    for k in range(1, rows):
        row_arrival(k).wait_recv()
    strip_sum = row_part[0]
    for k in range(1, rows):
        strip_sum = strip_sum + row_part[k]
    col_part[my_col] = strip_sum

    def col_share(k, slot):
        return pltpu.make_async_remote_copy(
            src_ref=col_part.at[my_col],
            dst_ref=col_part.at[slot],
            send_sem=csum_ss.at[k],
            recv_sem=csum_rs.at[slot],
            device_id=(my_row, col_peer(k)),
            device_id_type=MESH,
        )

    for k in range(1, cols):
        col_share(k, my_col).start()
    for k in range(1, cols):
        col_share(k, col_peer(k)).wait_recv()
    everything = col_part[0]
    for k in range(1, cols):
        everything = everything + col_part[k]
    everything = jnp.sum(everything, axis=1, keepdims=True)
    moments = [everything[m : m + 1, :] for m in range(2 * ITERS)]
    answer = solve_coefficients(moments)
    result = start_buf[0, GHOST : GHOST + high, 0:wide]
    for i, scale in enumerate(answer):
        result = result + scale * fields[i, GHOST : GHOST + high, 0:wide]
    heights[...] = result

    for side in (0, 1):
        @pl.when(has[side])
        def _(side=side):
            row_copy(side).wait_send()
            corner_copy(side).wait_send()

        pl.when(beside[side])(lambda side=side: col_copy(side).wait_send())
    for k in range(1, rows):
        row_share(k).wait_send()
    for k in range(1, cols):
        col_share(k, my_col).wait_send()


def local(counts, scatter_vectors, ground_ratio, vertical_wavenumber, initial_phase, initial_extinction):
    high, wide = initial_phase.shape
    rows, cols = counts
    vectors = scatter_vectors.reshape(RAW, high, wide)
    full = wide + LANES
    tall = high + 2 * GHOST
    edge = -(-(RAW * REACH + GUESS * GHOST) // 8) * 8
    packed = -(-(RAW + GUESS) * SLOT // LANES) * LANES
    vmem = pl.BlockSpec(memory_space=pltpu.VMEM)
    f32 = jnp.float32
    dma = pltpu.SemaphoreType.DMA
    out = jax.ShapeDtypeStruct((high, wide), f32)
    heights, extinction = pl.pallas_call(
        functools.partial(kernel, counts),
        out_shape=(out, out),
        in_specs=[pl.BlockSpec(memory_space=pltpu.HBM)] * 5,
        out_specs=(vmem, vmem),
        scratch_shapes=[
            pltpu.SMEM((CHANNELS,), f32),
            pltpu.VMEM((RAW, high, wide), f32),
            pltpu.VMEM((high, wide), f32),
            pltpu.VMEM((high, wide), f32),
            pltpu.VMEM((high, wide), f32),
            dma((5,)),
            pltpu.VMEM((2, edge, wide), f32),
            pltpu.VMEM((2, edge + 8, wide), f32),
            pltpu.VMEM((2, high, packed), f32),
            pltpu.VMEM((2, high, packed), f32),
            pltpu.VMEM((2, 2, SLOT, packed), f32),
            pltpu.VMEM((ITERS, tall, full), f32),
            pltpu.VMEM((GUESS, tall, full), f32),
            pltpu.VMEM((RAW, tall, full), f32),
            pltpu.VMEM((tall, full), f32),
            pltpu.VMEM((2, tall, full), f32),
            pltpu.VMEM((8, LANES), f32),
            pltpu.VMEM((rows, 8, LANES), f32),
            pltpu.VMEM((cols, 8, LANES), f32),
            dma((2,)), dma((2,)), dma((2,)), dma((2,)), dma((2,)), dma((2,)),
            dma((rows,)), dma((rows,)), dma((cols,)), dma((cols,)),
        ],
        compiler_params=pltpu.CompilerParams(
            collective_id=0, has_side_effects=True, vmem_limit_bytes=32 * 1024 * 1024
        ),
        cost_estimate=pl.CostEstimate(
            flops=2000 * high * wide, bytes_accessed=80 * high * wide, transcendentals=8 * high * wide
        ),
    )(ground_ratio, vectors, vertical_wavenumber, initial_phase, initial_extinction)
    return (heights, extinction)


def solution(mesh):
    placed = (
        P(None, None, None, "row", "col"),
        P(),
        P("row", "col"),
        P("row", "col"),
        P("row", "col"),
    )
    counts = (mesh.shape["row"], mesh.shape["col"])
    return jax.shard_map(
        functools.partial(local, counts),
        mesh=mesh,
        in_specs=placed,
        out_specs=(P("row", "col"), P("row", "col")),
        check_vma=False,
    )
```

```python
import functools

import jax
import jax.numpy as jnp
from jax import lax
from jax.experimental import pallas as pl
from jax.experimental.pallas import tpu as pltpu
from jax.sharding import PartitionSpec as P

RADIUS = 9
LAYERS = 16
GAUSS_STEPS = 2
ITERS = 3

EPSILON = 1e-06
DAMPING = 0.002
SMOOTHING = 1.0

CHANNELS = 3
RAW = 4 * CHANNELS
GUESS = 3
GHOST = ITERS + 1
REACH = RADIUS + GHOST
SLOT = 16
LANES = 128
SHIFT = 4.5 * SMOOTHING
MESH = pl.DeviceIdType.MESH


def turn(value, amount, axis):
    size = value.shape[axis]
    amount = amount % size
    return value if amount == 0 else pltpu.roll(value, amount, axis)


def window(value, axis):
    pair = value + turn(value, -1, axis)
    four = pair + turn(pair, -2, axis)
    eight = four + turn(four, -4, axis)
    most = eight + turn(eight, -8, axis)
    return most + turn(pair, -16, axis) + turn(value, -18, axis)


def sine_cosine(angle):
    square = angle * angle
    sine = -1.0 / 39916800.0 + square * (1.0 / 6227020800.0)
    for term in (362880.0, -5040.0, 120.0, -6.0):
        sine = sine * square + 1.0 / term
    sine = angle + angle * square * sine
    cosine = -1.0 / 3628800.0 + square * (1.0 / 479001600.0)
    for term in (40320.0, -720.0, 24.0, -2.0):
        cosine = cosine * square + 1.0 / term
    return sine, 1.0 + square * cosine


def volume_moments(phase, atten):
    sin_half, cos_half = sine_cosine(phase * (0.5 / LAYERS))
    sin_n = 2.0 * sin_half * cos_half
    cos_n = 1.0 - 2.0 * sin_half * sin_half
    grown = jnp.exp(atten * (1.0 / LAYERS))
    weight = 1.0 + grown
    depth = grown
    step_r = grown * cos_n
    step_i = grown * sin_n
    sum_r = 1.0 + step_r
    sum_i = step_i
    deep_r = step_r
    deep_i = step_i
    count = 2
    while count < LAYERS:
        sin_n, cos_n = 2.0 * sin_n * cos_n, 1.0 - 2.0 * sin_n * sin_n
        grown = jnp.exp(atten * (float(count) / LAYERS))
        step_r = grown * cos_n
        step_i = grown * sin_n
        depth = depth + grown * (depth + float(count) * weight)
        weight = weight + grown * weight
        inner_r = deep_r + float(count) * sum_r
        inner_i = deep_i + float(count) * sum_i
        deep_r = deep_r + (step_r * inner_r - step_i * inner_i)
        deep_i = deep_i + (step_r * inner_i + step_i * inner_r)
        sum_r, sum_i = (
            sum_r + (step_r * sum_r - step_i * sum_i),
            sum_i + (step_r * sum_i + step_i * sum_r),
        )
        count *= 2
    scale = 1.0 / weight
    fine = scale * (1.0 / LAYERS)
    deep_r = deep_r + 0.5 * sum_r
    deep_i = deep_i + 0.5 * sum_i
    return (
        depth * fine + 0.5 / LAYERS,
        (cos_half * sum_r - sin_half * sum_i) * scale,
        (cos_half * sum_i + sin_half * sum_r) * scale,
        (cos_half * deep_r - sin_half * deep_i) * fine,
        (cos_half * deep_i + sin_half * deep_r) * fine,
    )


def gauss_newton(phase, atten, known, weighted_re, weighted_im, weight_total, offset_total):
    for step in range(GAUSS_STEPS):
        if step > 0:
            known = volume_moments(phase, atten)
        mean, real, imag, depth_cos, depth_sin = known
        ra = depth_cos - mean * real
        rt = -depth_sin
        ia = depth_sin - mean * imag
        it = depth_cos
        er = weighted_re - weight_total * real - offset_total
        ei = weighted_im - weight_total * imag
        maa = weight_total * (ra * ra + ia * ia) + DAMPING
        map_ = weight_total * (ra * rt + ia * it)
        mpp = weight_total * (rt * rt + it * it) + DAMPING
        ga = ra * er + ia * ei
        gp = rt * er + it * ei
        over = 1.0 / (maa * mpp - map_ * map_)
        atten = atten + (mpp * ga - map_ * gp) * over
        phase = phase + (maa * gp - map_ * ga) * over
    return phase, atten


def dot_poly(left, right, moments):
    total = None
    for i, a in enumerate(left):
        for j, b in enumerate(right):
            term = a * b * moments[i + j]
            total = term if total is None else total + term
    return total


def add_poly(left, right, scale):
    size = max(len(left), len(right))
    out = []
    for i in range(size):
        if i >= len(right):
            out.append(left[i])
        elif i >= len(left):
            out.append(scale * right[i])
        else:
            out.append(left[i] + scale * right[i])
    return out


def solve_coefficients(moments):
    one = jnp.ones_like(moments[0])
    residual = [one]
    direction = [one]
    answer = []
    norm = moments[0]
    for iteration in range(ITERS):
        image = [SHIFT * d for d in direction] + [0.0 * one]
        for i, d in enumerate(direction):
            image[i + 1] = image[i + 1] + d
        step = norm / dot_poly(direction, image, moments)
        answer = add_poly(answer, direction, step)
        if iteration + 1 < ITERS:
            residual = add_poly(residual, image, -step)
            following = dot_poly(residual, residual, moments)
            direction = add_poly(residual, direction, following / norm)
            norm = following
    return answer


def kernel(
    counts, ratio_in, vectors_in, wavenumber_in, phase_in, atten_in, parts_out, answer_out,
    ratio, vectors, wavenumber, phase0, atten0, load_sem, store_sem, parts, first_fit, row_send, row_recv, col_send, col_recv, corner_recv, guess, sums,
    conf_buf, start_buf, mine, row_part, col_part,
    row_ss, row_rs, col_ss, col_rs, corner_ss, corner_rs, rsum_ss, rsum_rs, csum_ss, csum_rs,
):
    rows, cols = counts
    my_row = lax.axis_index("row")
    my_col = lax.axis_index("col")
    high, wide = phase0.shape
    full = wide + LANES
    tall = high + 2 * GHOST
    plain = (wavenumber, phase0, atten0)

    loads = [
        pltpu.make_async_copy(source, target, load_sem.at[i])
        for i, (source, target) in enumerate((
            (vectors_in, vectors), (wavenumber_in, wavenumber),
            (phase_in, phase0), (atten_in, atten0), (ratio_in, ratio),
        ))
    ]
    for load in loads:
        load.start()

    def row_peer(k):
        return lax.rem(my_row + k, rows)

    def col_peer(k):
        return lax.rem(my_col + k, cols)

    barrier = pltpu.get_barrier_semaphore()
    for k in range(1, rows):
        pl.semaphore_signal(barrier, inc=1, device_id=(row_peer(k), my_col), device_id_type=MESH)
    for k in range(1, cols):
        pl.semaphore_signal(barrier, inc=1, device_id=(my_row, col_peer(k)), device_id_type=MESH)

    has = (my_row > 0, my_row < rows - 1)
    beside = (my_col > 0, my_col < cols - 1)

    sent = row_send.shape[1]
    for side in (0, 1):
        row_recv[side, sent:, :] = jnp.zeros((row_recv.shape[1] - sent, wide), jnp.float32)
    first_row = GUESS * GHOST
    for load in loads:
        load.wait()
    for g in range(GUESS):
        row_send[0, g * GHOST : (g + 1) * GHOST, :] = plain[g][0:GHOST, :]
        row_send[1, g * GHOST : (g + 1) * GHOST, :] = plain[g][high - GHOST : high, :]
    for f in range(RAW):
        span = slice(first_row + f * REACH, first_row + (f + 1) * REACH)
        row_send[0, span, :] = vectors[f, 0:REACH, :]
        row_send[1, span, :] = vectors[f, high - REACH : high, :]

    def row_copy(side):
        return pltpu.make_async_remote_copy(
            src_ref=row_send.at[side],
            dst_ref=row_recv.at[1 - side, 0:sent, :],
            send_sem=row_ss.at[side],
            recv_sem=row_rs.at[1 - side],
            device_id=(my_row - 1 + 2 * side, my_col),
            device_id_type=MESH,
        )

    def col_copy(side):
        return pltpu.make_async_remote_copy(
            src_ref=col_send.at[side],
            dst_ref=col_recv.at[1 - side],
            send_sem=col_ss.at[side],
            recv_sem=col_rs.at[1 - side],
            device_id=(my_row, my_col - 1 + 2 * side),
            device_id_type=MESH,
        )

    def corner_copy(side):
        begin = 0 if side == 0 else high - SLOT
        return pltpu.make_async_remote_copy(
            src_ref=col_recv.at[:, begin : begin + SLOT, :],
            dst_ref=corner_recv.at[1 - side],
            send_sem=corner_ss.at[side],
            recv_sem=corner_rs.at[1 - side],
            device_id=(my_row - 1 + 2 * side, my_col),
            device_id_type=MESH,
        )

    pl.semaphore_wait(barrier, rows + cols - 2)
    for side in (0, 1):
        pl.when(has[side])(lambda side=side: row_copy(side).start())

    lane = lax.broadcasted_iota(jnp.int32, (high, LANES), 1)
    per = LANES // SLOT
    packs = (RAW + GUESS + per - 1) // per
    for k in range(packs):
        low = jnp.zeros((high, LANES), jnp.float32)
        top = jnp.zeros((high, LANES), jnp.float32)
        for p in range(per):
            f = k * per + p
            if f >= RAW + GUESS:
                continue
            if f < RAW:
                first, last = vectors[f, :, 0:LANES], vectors[f, :, wide - LANES : wide]
            else:
                ref = plain[f - RAW]
                first, last = ref[:, 0:LANES], ref[:, wide - LANES : wide]
            here = (lane >= p * SLOT) & (lane < (p + 1) * SLOT)
            low = jnp.where(here, turn(first, p * SLOT, 1), low)
            top = jnp.where(here, turn(last, (p + 1) * SLOT, 1), top)
        col_send[0, :, k * LANES : (k + 1) * LANES] = low
        col_send[1, :, k * LANES : (k + 1) * LANES] = top

    for side in (0, 1):
        pl.when(beside[side])(lambda side=side: col_copy(side).start())

    for side in (0, 1):
        @pl.when(jnp.logical_not(has[side]))
        def _(side=side):
            row_recv[side] = jnp.zeros(row_recv.shape[1:], jnp.float32)
            corner_recv[side] = jnp.zeros(corner_recv.shape[1:], jnp.float32)

        @pl.when(jnp.logical_not(beside[side]))
        def _(side=side):
            col_recv[side] = jnp.zeros(col_recv.shape[1:], jnp.float32)

    def products(raws):
        re1, im1, re2, im2 = raws
        return (
            re1 * re1 + im1 * im1,
            re2 * re2 + im2 * im2,
            re1 * re2 + im1 * im2,
            re1 * im2 - im1 * re2,
        )

    deep = -(-(2 * REACH + high) // 8) * 8
    above_own = jnp.zeros((REACH, LANES), jnp.float32)
    below_own = jnp.zeros((deep - REACH - high, LANES), jnp.float32)

    def own_sums(channel, raws, piece):
        for i, product in enumerate(products(raws)):
            placed = jnp.concatenate([above_own, product, below_own], axis=0)
            sums[4 * channel + i, :, piece] = window(placed, 0)[0:tall, :]

    def inner_sums(channel, carry):
        for strip in range(wide // LANES):
            piece = slice(strip * LANES, (strip + 1) * LANES)
            own_sums(channel, [vectors[CHANNELS * i + channel, :, piece] for i in range(4)], piece)
        return carry

    lax.fori_loop(0, CHANNELS, inner_sums, 0)
    for g in range(GUESS):
        guess[g, GHOST : GHOST + high, 0:wide] = plain[g][...]

    for side in (0, 1):
        pl.when(beside[side])(lambda side=side: col_copy(1 - side).wait_recv())
    for side in (0, 1):
        pl.when(has[side])(lambda side=side: corner_copy(side).start())

    def unpacked(left, right, f):
        p = f % per
        place = lax.broadcasted_iota(jnp.int32, left.shape, 1)
        return jnp.where(
            place < LANES // 2,
            turn(right, -p * SLOT, 1),
            turn(left, LANES - SLOT - p * SLOT, 1),
        )

    def outer(f):
        piece = slice(f // per * LANES, (f // per + 1) * LANES)
        return unpacked(col_recv[0, :, piece], col_recv[1, :, piece], f)

    for channel in range(CHANNELS):
        own_sums(channel, [outer(CHANNELS * i + channel) for i in range(4)], slice(wide, full))
    for g in range(GUESS):
        guess[g, GHOST : GHOST + high, wide:full] = outer(RAW + g)

    ratios = [jnp.full((1, full), ratio[k], jnp.float32) for k in range(CHANNELS)]
    weights = [1.0 / (1.0 + r) for r in ratios]
    weight_total = sum(w * w for w in weights)
    offset_total = sum(r * w * w for r, w in zip(ratios, weights))

    def fit(chunk):
        block = pl.ds(pl.multiple_of(chunk * 8, 8), 8)
        found = None
        for k in range(CHANNELS):
            power1, power2, cross_re, cross_im = [
                window(sums[4 * k + i, block, :], 1) for i in range(4)
            ]
            scale = lax.rsqrt(power1 * power2 + EPSILON)
            real = cross_re * scale
            imag = cross_im * scale
            parts = (real * weights[k], imag * weights[k], real * real + imag * imag)
            found = parts if k == 0 else [a + b for a, b in zip(found, parts)]
        weighted_re, weighted_im, confidence = [turn(a, RADIUS, 1) for a in found]
        phase, atten = gauss_newton(
            guess[1, block, :], guess[2, block, :], [first_fit[i, block, :] for i in range(5)],
            weighted_re, weighted_im, weight_total, offset_total,
        )
        conf_buf[block, :] = confidence * (1.0 / CHANNELS)
        start_buf[0, block, :] = phase / guess[0, block, :]
        start_buf[1, block, :] = atten

    for g in range(GUESS):
        guess[g, 0:GHOST, :] = jnp.zeros((GHOST, full), jnp.float32)
        guess[g, GHOST + high : tall, :] = jnp.zeros((GHOST, full), jnp.float32)

    def guessed(chunk, carry):
        block = pl.ds(pl.multiple_of(chunk * 8, 8), 8)
        for i, moment in enumerate(volume_moments(guess[1, block, :], guess[2, block, :])):
            first_fit[i, block, :] = moment
        return carry

    chunks = tall // 8
    edge_chunks = SLOT // 8

    def middle(chunk, carry):
        fit(chunk)
        return carry

    lax.fori_loop(0, chunks, guessed, 0)
    lax.fori_loop(edge_chunks, chunks - edge_chunks, middle, 0)

    for side in (0, 1):
        @pl.when(has[side])
        def _(side=side):
            row_copy(1 - side).wait_recv()
            corner_copy(1 - side).wait_recv()

    line = lax.broadcasted_iota(jnp.int32, (SLOT, LANES), 0)
    keep = (line < REACH, line >= SLOT - REACH)

    def running(value, down):
        for k in (1, 2, 4, 8):
            if down:
                value = value + jnp.where(line >= k, turn(value, k, 0), 0.0)
            else:
                value = value + jnp.where(line < SLOT - k, turn(value, -k, 0), 0.0)
        return value

    def corner(side, f):
        piece = slice(f // per * LANES, (f // per + 1) * LANES)
        return unpacked(corner_recv[side, 0, :, piece], corner_recv[side, 1, :, piece], f)

    def halo_rows(side, f, strip):
        if strip < wide // LANES:
            begin = first_row + f * REACH - side * (SLOT - REACH)
            value = row_recv[side, begin : begin + SLOT, strip * LANES : (strip + 1) * LANES]
        else:
            value = turn(corner(side, f), (1 - 2 * side) * (REACH - SLOT), 0)
        return jnp.where(keep[side], value, 0.0)

    for side in (0, 1):
        begin = side * (tall - SLOT)
        for channel in range(CHANNELS):
            for strip in range(full // LANES):
                piece = slice(strip * LANES, (strip + 1) * LANES)
                raws = [halo_rows(side, CHANNELS * i + channel, strip) for i in range(4)]
                for i, product in enumerate(products(raws)):
                    sums[4 * channel + i, begin : begin + SLOT, piece] += running(product, side == 1)
    for g in range(GUESS):
        span = slice(g * GHOST, (g + 1) * GHOST)
        guess[g, 0:GHOST, 0:wide] = row_recv[0, span, :]
        guess[g, GHOST + high : tall, 0:wide] = row_recv[1, span, :]
        guess[g, 0:GHOST, wide:full] = corner(0, RAW + g)[SLOT - GHOST :, :]
        guess[g, GHOST + high : tall, wide:full] = corner(1, RAW + g)[0:GHOST, :]

    ghosts = [
        jnp.concatenate([guess[g, 0:GHOST, :], guess[g, GHOST + high : tall, :]], axis=0) for g in (1, 2)
    ]
    for i, moment in enumerate(volume_moments(*ghosts)):
        first_fit[i, 0:GHOST, :] = moment[0:GHOST, :]
        first_fit[i, GHOST + high : tall, :] = moment[GHOST : 2 * GHOST, :]

    def edges(step, carry):
        fit(step + step // edge_chunks * (chunks - 2 * edge_chunks))
        return carry

    lax.fori_loop(0, 2 * edge_chunks, edges, 0)

    row_at = lax.broadcasted_iota(jnp.int32, (tall, full), 0) - GHOST
    lane_at = lax.broadcasted_iota(jnp.int32, (tall, full), 1)
    col_at = jnp.where(lane_at < wide + LANES // 2, lane_at, lane_at - full)
    near = (col_at >= -GHOST) & (col_at < wide + GHOST)
    row_all = row_at + my_row * high
    col_all = col_at + my_col * wide
    inside = near & (row_all >= 0) & (row_all < rows * high) & (col_all >= 0) & (col_all < cols * wide)

    def masked(value):
        return jnp.where(inside, value, 0.0)

    def around(value):
        return turn(value, 1, 0) + turn(value, -1, 0) + turn(value, 1, 1) + turn(value, -1, 1)

    start = masked(start_buf[0])
    confidence = conf_buf[...]
    centred = confidence + (4.0 * SMOOTHING - SHIFT)
    basis = [masked(SMOOTHING * (around(start) - 4.0 * start))]
    for _ in range(ITERS - 1):
        basis.append(masked(centred * basis[-1] - SMOOTHING * around(basis[-1])))
    basis.append(centred * basis[-1] - SMOOTHING * around(basis[-1]))

    parts[0] = start[GHOST : GHOST + high, 0:wide]
    for i in range(ITERS):
        parts[1 + i] = basis[i][GHOST : GHOST + high, 0:wide]
    parts[1 + ITERS] = start_buf[1, GHOST : GHOST + high, 0:wide]
    store = pltpu.make_async_copy(parts, parts_out, store_sem)
    own = inside & (row_at >= 0) & (row_at < high) & (lane_at < wide)
    for m in range(2 * ITERS):
        product = jnp.where(own, basis[m // 2] * basis[m - m // 2], 0.0)
        line = jnp.sum(product, axis=0, keepdims=True)
        total = line[:, 0:LANES]
        for strip in range(1, wide // LANES):
            total = total + line[:, strip * LANES : (strip + 1) * LANES]
        mine[m : m + 1, :] = total
    mine[2 * ITERS :, :] = jnp.zeros((8 - 2 * ITERS, LANES), jnp.float32)

    def row_share(k):
        return pltpu.make_async_remote_copy(
            src_ref=mine,
            dst_ref=row_part.at[my_row],
            send_sem=rsum_ss.at[k],
            recv_sem=rsum_rs.at[my_row],
            device_id=(row_peer(k), my_col),
            device_id_type=MESH,
        )

    def row_arrival(k):
        who = row_peer(k)
        return pltpu.make_async_remote_copy(
            src_ref=mine,
            dst_ref=row_part.at[who],
            send_sem=rsum_ss.at[k],
            recv_sem=rsum_rs.at[who],
            device_id=(who, my_col),
            device_id_type=MESH,
        )

    for k in range(1, rows):
        row_share(k).start()
    store.start()
    row_part[my_row] = mine[...]
    for k in range(1, rows):
        row_arrival(k).wait_recv()
    strip_sum = row_part[0]
    for k in range(1, rows):
        strip_sum = strip_sum + row_part[k]
    col_part[my_col] = strip_sum

    def col_share(k, slot):
        return pltpu.make_async_remote_copy(
            src_ref=col_part.at[my_col],
            dst_ref=col_part.at[slot],
            send_sem=csum_ss.at[k],
            recv_sem=csum_rs.at[slot],
            device_id=(my_row, col_peer(k)),
            device_id_type=MESH,
        )

    for k in range(1, cols):
        col_share(k, my_col).start()
    for k in range(1, cols):
        col_share(k, col_peer(k)).wait_recv()
    everything = col_part[0]
    for k in range(1, cols):
        everything = everything + col_part[k]
    everything = jnp.sum(everything, axis=1, keepdims=True)
    moments = [everything[m : m + 1, :] for m in range(2 * ITERS)]
    answer = solve_coefficients(moments)
    for i, scale in enumerate(answer):
        answer_out[i : i + 1, :] = jnp.broadcast_to(scale, (1, wide))
    answer_out[ITERS:, :] = jnp.zeros((8 - ITERS, wide), jnp.float32)
    store.wait()

    for side in (0, 1):
        @pl.when(has[side])
        def _(side=side):
            row_copy(side).wait_send()
            corner_copy(side).wait_send()

        pl.when(beside[side])(lambda side=side: col_copy(side).wait_send())
    for k in range(1, rows):
        row_share(k).wait_send()
    for k in range(1, cols):
        col_share(k, my_col).wait_send()


def local(counts, scatter_vectors, ground_ratio, vertical_wavenumber, initial_phase, initial_extinction):
    high, wide = initial_phase.shape
    rows, cols = counts
    vectors = scatter_vectors.reshape(RAW, high, wide)
    full = wide + LANES
    tall = high + 2 * GHOST
    edge = -(-(RAW * REACH + GUESS * GHOST) // 8) * 8
    packed = -(-(RAW + GUESS) * SLOT // LANES) * LANES
    vmem = pl.BlockSpec(memory_space=pltpu.VMEM)
    f32 = jnp.float32
    dma = pltpu.SemaphoreType.DMA
    out = (
        jax.ShapeDtypeStruct((2 + ITERS, high, wide), f32),
        jax.ShapeDtypeStruct((8, wide), f32),
    )
    parts, answer = pl.pallas_call(
        functools.partial(kernel, counts),
        out_shape=out,
        in_specs=[pl.BlockSpec(memory_space=pltpu.HBM)] * 5,
        out_specs=(pl.BlockSpec(memory_space=pltpu.HBM), vmem),
        scratch_shapes=[
            pltpu.SMEM((CHANNELS,), f32),
            pltpu.VMEM((RAW, high, wide), f32),
            pltpu.VMEM((high, wide), f32),
            pltpu.VMEM((high, wide), f32),
            pltpu.VMEM((high, wide), f32),
            dma((5,)),
            dma(()),
            pltpu.VMEM((2 + ITERS, high, wide), f32),
            pltpu.VMEM((5, tall, full), f32),
            pltpu.VMEM((2, edge, wide), f32),
            pltpu.VMEM((2, edge + 8, wide), f32),
            pltpu.VMEM((2, high, packed), f32),
            pltpu.VMEM((2, high, packed), f32),
            pltpu.VMEM((2, 2, SLOT, packed), f32),
            pltpu.VMEM((GUESS, tall, full), f32),
            pltpu.VMEM((RAW, tall, full), f32),
            pltpu.VMEM((tall, full), f32),
            pltpu.VMEM((2, tall, full), f32),
            pltpu.VMEM((8, LANES), f32),
            pltpu.VMEM((rows, 8, LANES), f32),
            pltpu.VMEM((cols, 8, LANES), f32),
            dma((2,)), dma((2,)), dma((2,)), dma((2,)), dma((2,)), dma((2,)),
            dma((rows,)), dma((rows,)), dma((cols,)), dma((cols,)),
        ],
        compiler_params=pltpu.CompilerParams(
            collective_id=0, has_side_effects=True, vmem_limit_bytes=56 * 1024 * 1024
        ),
        cost_estimate=pl.CostEstimate(
            flops=2000 * high * wide, bytes_accessed=80 * high * wide, transcendentals=8 * high * wide
        ),
    )(ground_ratio, vectors, vertical_wavenumber, initial_phase, initial_extinction)
    heights = parts[0]
    for i in range(ITERS):
        heights = heights + answer[i : i + 1, :] * parts[1 + i]
    return (heights, parts[1 + ITERS])


def solution(mesh):
    placed = (
        P(None, None, None, "row", "col"),
        P(),
        P("row", "col"),
        P("row", "col"),
        P("row", "col"),
    )
    counts = (mesh.shape["row"], mesh.shape["col"])
    return jax.shard_map(
        functools.partial(local, counts),
        mesh=mesh,
        in_specs=placed,
        out_specs=(P("row", "col"), P("row", "col")),
        check_vma=False,
    )
```

```python
import functools

import jax
import jax.numpy as jnp
from jax import lax
from jax.experimental import pallas as pl
from jax.experimental.pallas import tpu as pltpu
from jax.sharding import PartitionSpec as P

RADIUS = 9
LAYERS = 16
GAUSS_STEPS = 2
ITERS = 3

EPSILON = 1e-06
DAMPING = 0.002
SMOOTHING = 1.0

CHANNELS = 3
RAW = 4 * CHANNELS
GUESS = 3
GHOST = ITERS + 1
REACH = RADIUS + GHOST
SLOT = 16
LANES = 128
SHIFT = 4.5 * SMOOTHING
MESH = pl.DeviceIdType.MESH


def turn(value, amount, axis):
    size = value.shape[axis]
    amount = amount % size
    return value if amount == 0 else pltpu.roll(value, amount, axis)


def window(value, axis):
    pair = value + turn(value, -1, axis)
    four = pair + turn(pair, -2, axis)
    eight = four + turn(four, -4, axis)
    most = eight + turn(eight, -8, axis)
    return most + turn(pair, -16, axis) + turn(value, -18, axis)


def sine_cosine(angle):
    square = angle * angle
    sine = -1.0 / 39916800.0 + square * (1.0 / 6227020800.0)
    for term in (362880.0, -5040.0, 120.0, -6.0):
        sine = sine * square + 1.0 / term
    sine = angle + angle * square * sine
    cosine = -1.0 / 3628800.0 + square * (1.0 / 479001600.0)
    for term in (40320.0, -720.0, 24.0, -2.0):
        cosine = cosine * square + 1.0 / term
    return sine, 1.0 + square * cosine


def volume_moments(phase, atten):
    sin_half, cos_half = sine_cosine(phase * (0.5 / LAYERS))
    sin_n = 2.0 * sin_half * cos_half
    cos_n = 1.0 - 2.0 * sin_half * sin_half
    grown = jnp.exp(atten * (1.0 / LAYERS))
    weight = 1.0 + grown
    depth = grown
    step_r = grown * cos_n
    step_i = grown * sin_n
    sum_r = 1.0 + step_r
    sum_i = step_i
    deep_r = step_r
    deep_i = step_i
    count = 2
    while count < LAYERS:
        sin_n, cos_n = 2.0 * sin_n * cos_n, 1.0 - 2.0 * sin_n * sin_n
        grown = jnp.exp(atten * (float(count) / LAYERS))
        step_r = grown * cos_n
        step_i = grown * sin_n
        depth = depth + grown * (depth + float(count) * weight)
        weight = weight + grown * weight
        inner_r = deep_r + float(count) * sum_r
        inner_i = deep_i + float(count) * sum_i
        deep_r = deep_r + (step_r * inner_r - step_i * inner_i)
        deep_i = deep_i + (step_r * inner_i + step_i * inner_r)
        sum_r, sum_i = (
            sum_r + (step_r * sum_r - step_i * sum_i),
            sum_i + (step_r * sum_i + step_i * sum_r),
        )
        count *= 2
    scale = 1.0 / weight
    fine = scale * (1.0 / LAYERS)
    deep_r = deep_r + 0.5 * sum_r
    deep_i = deep_i + 0.5 * sum_i
    return (
        depth * fine + 0.5 / LAYERS,
        (cos_half * sum_r - sin_half * sum_i) * scale,
        (cos_half * sum_i + sin_half * sum_r) * scale,
        (cos_half * deep_r - sin_half * deep_i) * fine,
        (cos_half * deep_i + sin_half * deep_r) * fine,
    )


def gauss_newton(phase, atten, known, weighted_re, weighted_im, weight_total, offset_total):
    for step in range(GAUSS_STEPS):
        if step > 0:
            known = volume_moments(phase, atten)
        mean, real, imag, depth_cos, depth_sin = known
        ra = depth_cos - mean * real
        rt = -depth_sin
        ia = depth_sin - mean * imag
        it = depth_cos
        er = weighted_re - weight_total * real - offset_total
        ei = weighted_im - weight_total * imag
        maa = weight_total * (ra * ra + ia * ia) + DAMPING
        map_ = weight_total * (ra * rt + ia * it)
        mpp = weight_total * (rt * rt + it * it) + DAMPING
        ga = ra * er + ia * ei
        gp = rt * er + it * ei
        over = 1.0 / (maa * mpp - map_ * map_)
        atten = atten + (mpp * ga - map_ * gp) * over
        phase = phase + (maa * gp - map_ * ga) * over
    return phase, atten


def dot_poly(left, right, moments):
    total = None
    for i, a in enumerate(left):
        for j, b in enumerate(right):
            term = a * b * moments[i + j]
            total = term if total is None else total + term
    return total


def add_poly(left, right, scale):
    size = max(len(left), len(right))
    out = []
    for i in range(size):
        if i >= len(right):
            out.append(left[i])
        elif i >= len(left):
            out.append(scale * right[i])
        else:
            out.append(left[i] + scale * right[i])
    return out


def solve_coefficients(moments):
    one = jnp.ones_like(moments[0])
    residual = [one]
    direction = [one]
    answer = []
    norm = moments[0]
    for iteration in range(ITERS):
        image = [SHIFT * d for d in direction] + [0.0 * one]
        for i, d in enumerate(direction):
            image[i + 1] = image[i + 1] + d
        step = norm / dot_poly(direction, image, moments)
        answer = add_poly(answer, direction, step)
        if iteration + 1 < ITERS:
            residual = add_poly(residual, image, -step)
            following = dot_poly(residual, residual, moments)
            direction = add_poly(residual, direction, following / norm)
            norm = following
    return answer


def kernel(
    counts, edges_at, ratio_in, vectors_in, wavenumber_in, phase_in, atten_in, parts_out,
    ratio, vectors, wavenumber, phase0, atten0, load_sem, store_sem, results, mixed, parts, first_fit, row_send, row_recv, col_send, col_recv, corner_recv, guess, sums,
    conf_buf, start_buf, mine, row_part, col_part,
    row_ss, row_rs, col_ss, col_rs, corner_ss, corner_rs, rsum_ss, rsum_rs, csum_ss, csum_rs,
):
    rows, cols = counts
    my_row = lax.axis_index("row")
    my_col = lax.axis_index("col")
    high, wide = phase0.shape
    full = wide + LANES
    tall = high + 2 * GHOST
    plain = (wavenumber, phase0, atten0)

    loads = [
        pltpu.make_async_copy(source, target, load_sem.at[i])
        for i, (source, target) in enumerate((
            (vectors_in, vectors), (wavenumber_in, wavenumber),
            (phase_in, phase0), (atten_in, atten0), (ratio_in, ratio),
        ))
    ]
    for load in loads:
        load.start()

    def row_peer(k):
        return lax.rem(my_row + k, rows)

    def col_peer(k):
        return lax.rem(my_col + k, cols)

    barrier = pltpu.get_barrier_semaphore()
    for k in range(1, rows):
        pl.semaphore_signal(barrier, inc=1, device_id=(row_peer(k), my_col), device_id_type=MESH)
    for k in range(1, cols):
        pl.semaphore_signal(barrier, inc=1, device_id=(my_row, col_peer(k)), device_id_type=MESH)

    has = (my_row > 0, my_row < rows - 1)
    beside = (my_col > 0, my_col < cols - 1)

    for side in (0, 1):
        for channel in range(CHANNELS):
            used = edges_at[channel] + 4 * REACH + (GUESS * GHOST if channel == 0 else 0)
            if used < edges_at[channel + 1]:
                spare = edges_at[channel + 1] - used
                row_send[side, used : edges_at[channel + 1], :] = jnp.zeros((spare, wide), jnp.float32)

    lead = (GUESS - 1) * GHOST

    def row_begin(f):
        channel, i = f % CHANNELS, f // CHANNELS
        return edges_at[channel] + (lead if channel == 0 else 0) + i * REACH

    def guess_rows(g):
        begin = g * GHOST if g < GUESS - 1 else lead + 4 * REACH
        return slice(begin, begin + GHOST)

    for load in loads:
        load.wait()
    for g in range(GUESS):
        row_send[0, guess_rows(g), :] = plain[g][0:GHOST, :]
        row_send[1, guess_rows(g), :] = plain[g][high - GHOST : high, :]
    for f in range(RAW):
        span = slice(row_begin(f), row_begin(f) + REACH)
        row_send[0, span, :] = vectors[f, 0:REACH, :]
        row_send[1, span, :] = vectors[f, high - REACH : high, :]

    def row_copy(side, channel):
        span = slice(edges_at[channel], edges_at[channel + 1])
        return pltpu.make_async_remote_copy(
            src_ref=row_send.at[side, span, :],
            dst_ref=row_recv.at[1 - side, span, :],
            send_sem=row_ss.at[side, channel],
            recv_sem=row_rs.at[1 - side, channel],
            device_id=(my_row - 1 + 2 * side, my_col),
            device_id_type=MESH,
        )

    def col_copy(side):
        return pltpu.make_async_remote_copy(
            src_ref=col_send.at[side],
            dst_ref=col_recv.at[1 - side],
            send_sem=col_ss.at[side],
            recv_sem=col_rs.at[1 - side],
            device_id=(my_row, my_col - 1 + 2 * side),
            device_id_type=MESH,
        )

    def corner_copy(side):
        begin = 0 if side == 0 else high - SLOT
        return pltpu.make_async_remote_copy(
            src_ref=col_recv.at[:, begin : begin + SLOT, :],
            dst_ref=corner_recv.at[1 - side],
            send_sem=corner_ss.at[side],
            recv_sem=corner_rs.at[1 - side],
            device_id=(my_row - 1 + 2 * side, my_col),
            device_id_type=MESH,
        )

    pl.semaphore_wait(barrier, rows + cols - 2)
    for channel in range(CHANNELS - 1):
        for side in (0, 1):
            pl.when(has[side])(lambda side=side, channel=channel: row_copy(side, channel).start())

    lane = lax.broadcasted_iota(jnp.int32, (high, LANES), 1)
    per = LANES // SLOT
    packs = (RAW + GUESS + per - 1) // per
    for k in range(packs):
        low = jnp.zeros((high, LANES), jnp.float32)
        top = jnp.zeros((high, LANES), jnp.float32)
        for p in range(per):
            f = k * per + p
            if f >= RAW + GUESS:
                continue
            if f < RAW:
                first, last = vectors[f, :, 0:LANES], vectors[f, :, wide - LANES : wide]
            else:
                ref = plain[f - RAW]
                first, last = ref[:, 0:LANES], ref[:, wide - LANES : wide]
            here = (lane >= p * SLOT) & (lane < (p + 1) * SLOT)
            low = jnp.where(here, turn(first, p * SLOT, 1), low)
            top = jnp.where(here, turn(last, (p + 1) * SLOT, 1), top)
        col_send[0, :, k * LANES : (k + 1) * LANES] = low
        col_send[1, :, k * LANES : (k + 1) * LANES] = top

    for side in (0, 1):
        pl.when(beside[side])(lambda side=side: col_copy(side).start())

    for side in (0, 1):
        @pl.when(jnp.logical_not(has[side]))
        def _(side=side):
            row_recv[side] = jnp.zeros(row_recv.shape[1:], jnp.float32)
            corner_recv[side] = jnp.zeros(corner_recv.shape[1:], jnp.float32)

        @pl.when(jnp.logical_not(beside[side]))
        def _(side=side):
            col_recv[side] = jnp.zeros(col_recv.shape[1:], jnp.float32)

    def products(raws):
        re1, im1, re2, im2 = raws
        return (
            re1 * re1 + im1 * im1,
            re2 * re2 + im2 * im2,
            re1 * re2 + im1 * im2,
            re1 * im2 - im1 * re2,
        )

    deep = -(-(2 * REACH + high) // 8) * 8
    above_own = jnp.zeros((REACH, LANES), jnp.float32)
    below_own = jnp.zeros((deep - REACH - high, LANES), jnp.float32)

    def own_sums(channel, raws, piece):
        for i, product in enumerate(products(raws)):
            placed = jnp.concatenate([above_own, product, below_own], axis=0)
            sums[4 * channel + i, :, piece] = window(placed, 0)[0:tall, :]

    def inner_sums(channel, carry):
        for strip in range(wide // LANES):
            piece = slice(strip * LANES, (strip + 1) * LANES)
            own_sums(channel, [vectors[CHANNELS * i + channel, :, piece] for i in range(4)], piece)
        return carry

    lax.fori_loop(0, CHANNELS, inner_sums, 0)
    for g in range(GUESS):
        guess[g, GHOST : GHOST + high, 0:wide] = plain[g][...]

    for side in (0, 1):
        pl.when(beside[side])(lambda side=side: col_copy(1 - side).wait_recv())
    for side in (0, 1):
        pl.when(has[side])(lambda side=side: corner_copy(side).start())
    for side in (0, 1):
        pl.when(has[side])(lambda side=side: row_copy(side, CHANNELS - 1).start())

    def unpacked(left, right, f):
        p = f % per
        place = lax.broadcasted_iota(jnp.int32, left.shape, 1)
        return jnp.where(
            place < LANES // 2,
            turn(right, -p * SLOT, 1),
            turn(left, LANES - SLOT - p * SLOT, 1),
        )

    def outer(f):
        piece = slice(f // per * LANES, (f // per + 1) * LANES)
        return unpacked(col_recv[0, :, piece], col_recv[1, :, piece], f)

    for channel in range(CHANNELS):
        own_sums(channel, [outer(CHANNELS * i + channel) for i in range(4)], slice(wide, full))
    for g in range(GUESS):
        guess[g, GHOST : GHOST + high, wide:full] = outer(RAW + g)

    ratios = [jnp.full((1, full), ratio[k], jnp.float32) for k in range(CHANNELS)]
    weights = [1.0 / (1.0 + r) for r in ratios]
    weight_total = sum(w * w for w in weights)
    offset_total = sum(r * w * w for r, w in zip(ratios, weights))

    def cohere(channel, chunk):
        block = pl.ds(pl.multiple_of(chunk * 8, 8), 8)
        power1, power2, cross_re, cross_im = [
            window(sums[4 * channel + i, block, :], 1) for i in range(4)
        ]
        scale = lax.rsqrt(power1 * power2 + EPSILON)
        real = cross_re * scale
        imag = cross_im * scale
        found = (real * weights[channel], imag * weights[channel], real * real + imag * imag)
        for i, value in enumerate(found):
            if channel == 0:
                mixed[i, block, :] = value
            else:
                mixed[i, block, :] += value

    def fit(chunk):
        block = pl.ds(pl.multiple_of(chunk * 8, 8), 8)
        weighted_re, weighted_im, confidence = [turn(mixed[i, block, :], RADIUS, 1) for i in range(3)]
        phase, atten = gauss_newton(
            guess[1, block, :], guess[2, block, :], [first_fit[i, block, :] for i in range(5)],
            weighted_re, weighted_im, weight_total, offset_total,
        )
        conf_buf[block, :] = confidence * (1.0 / CHANNELS)
        start_buf[0, block, :] = phase / guess[0, block, :]
        start_buf[1, block, :] = atten

    for g in range(GUESS):
        guess[g, 0:GHOST, :] = jnp.zeros((GHOST, full), jnp.float32)
        guess[g, GHOST + high : tall, :] = jnp.zeros((GHOST, full), jnp.float32)

    def guessed(chunk, carry):
        block = pl.ds(pl.multiple_of(chunk * 8, 8), 8)
        for i, moment in enumerate(volume_moments(guess[1, block, :], guess[2, block, :])):
            first_fit[i, block, :] = moment
        return carry

    chunks = tall // 8
    edge_chunks = SLOT // 8

    def middle(chunk, carry):
        for channel in range(CHANNELS):
            cohere(channel, chunk)
        fit(chunk)
        return carry

    lax.fori_loop(0, chunks, guessed, 0)
    lax.fori_loop(edge_chunks, chunks - edge_chunks, middle, 0)

    line = lax.broadcasted_iota(jnp.int32, (SLOT, LANES), 0)
    keep = (line < REACH, line >= SLOT - REACH)

    def running(value, down):
        for k in (1, 2, 4, 8):
            if down:
                value = value + jnp.where(line >= k, turn(value, k, 0), 0.0)
            else:
                value = value + jnp.where(line < SLOT - k, turn(value, -k, 0), 0.0)
        return value

    def corner(side, f):
        piece = slice(f // per * LANES, (f // per + 1) * LANES)
        return unpacked(corner_recv[side, 0, :, piece], corner_recv[side, 1, :, piece], f)

    def halo_rows(side, f, strip):
        if strip < wide // LANES:
            begin = row_begin(f) - side * (SLOT - REACH)
            value = row_recv[side, begin : begin + SLOT, strip * LANES : (strip + 1) * LANES]
        else:
            value = turn(corner(side, f), (1 - 2 * side) * (REACH - SLOT), 0)
        return jnp.where(keep[side], value, 0.0)

    def edge_chunk(step):
        return step + step // edge_chunks * (chunks - 2 * edge_chunks)

    for channel in range(CHANNELS):
        for side in (0, 1):
            @pl.when(has[side])
            def _(side=side, channel=channel):
                row_copy(1 - side, channel).wait_recv()
                if channel == 0:
                    corner_copy(1 - side).wait_recv()

        for side in (0, 1):
            begin = side * (tall - SLOT)
            for strip in range(full // LANES):
                piece = slice(strip * LANES, (strip + 1) * LANES)
                raws = [halo_rows(side, CHANNELS * i + channel, strip) for i in range(4)]
                for i, product in enumerate(products(raws)):
                    sums[4 * channel + i, begin : begin + SLOT, piece] += running(product, side == 1)

        def edge_cohere(step, carry, channel=channel):
            cohere(channel, edge_chunk(step))
            return carry

        lax.fori_loop(0, 2 * edge_chunks, edge_cohere, 0)
        if channel == 0:
            for g in range(GUESS):
                span = guess_rows(g)
                guess[g, 0:GHOST, 0:wide] = row_recv[0, span, :]
                guess[g, GHOST + high : tall, 0:wide] = row_recv[1, span, :]
                guess[g, 0:GHOST, wide:full] = corner(0, RAW + g)[SLOT - GHOST :, :]
                guess[g, GHOST + high : tall, wide:full] = corner(1, RAW + g)[0:GHOST, :]

            ghosts = [
                jnp.concatenate([guess[g, 0:GHOST, :], guess[g, GHOST + high : tall, :]], axis=0) for g in (1, 2)
            ]
            for i, moment in enumerate(volume_moments(*ghosts)):
                first_fit[i, 0:GHOST, :] = moment[0:GHOST, :]
                first_fit[i, GHOST + high : tall, :] = moment[GHOST : 2 * GHOST, :]

    def edges(step, carry):
        fit(edge_chunk(step))
        return carry

    lax.fori_loop(0, 2 * edge_chunks, edges, 0)

    row_at = lax.broadcasted_iota(jnp.int32, (tall, full), 0) - GHOST
    lane_at = lax.broadcasted_iota(jnp.int32, (tall, full), 1)
    col_at = jnp.where(lane_at < wide + LANES // 2, lane_at, lane_at - full)
    near = (col_at >= -GHOST) & (col_at < wide + GHOST)
    row_all = row_at + my_row * high
    col_all = col_at + my_col * wide
    inside = near & (row_all >= 0) & (row_all < rows * high) & (col_all >= 0) & (col_all < cols * wide)

    def masked(value):
        return jnp.where(inside, value, 0.0)

    def around(value):
        return turn(value, 1, 0) + turn(value, -1, 0) + turn(value, 1, 1) + turn(value, -1, 1)

    start = masked(start_buf[0])
    confidence = conf_buf[...]
    centred = confidence + (4.0 * SMOOTHING - SHIFT)
    basis = [masked(SMOOTHING * (around(start) - 4.0 * start))]
    for _ in range(ITERS - 1):
        basis.append(masked(centred * basis[-1] - SMOOTHING * around(basis[-1])))
    basis.append(centred * basis[-1] - SMOOTHING * around(basis[-1]))

    parts[0] = start[GHOST : GHOST + high, 0:wide]
    for i in range(ITERS):
        parts[1 + i] = basis[i][GHOST : GHOST + high, 0:wide]
    results[1] = start_buf[1, GHOST : GHOST + high, 0:wide]

    def store(i):
        return pltpu.make_async_copy(results.at[i], parts_out.at[i], store_sem.at[i])

    own = inside & (row_at >= 0) & (row_at < high) & (lane_at < wide)
    for m in range(2 * ITERS):
        product = jnp.where(own, basis[m // 2] * basis[m - m // 2], 0.0)
        line = jnp.sum(product, axis=0, keepdims=True)
        total = line[:, 0:LANES]
        for strip in range(1, wide // LANES):
            total = total + line[:, strip * LANES : (strip + 1) * LANES]
        mine[m : m + 1, :] = total
    mine[2 * ITERS :, :] = jnp.zeros((8 - 2 * ITERS, LANES), jnp.float32)

    def row_share(k):
        return pltpu.make_async_remote_copy(
            src_ref=mine,
            dst_ref=row_part.at[my_row],
            send_sem=rsum_ss.at[k],
            recv_sem=rsum_rs.at[my_row],
            device_id=(row_peer(k), my_col),
            device_id_type=MESH,
        )

    def row_arrival(k):
        who = row_peer(k)
        return pltpu.make_async_remote_copy(
            src_ref=mine,
            dst_ref=row_part.at[who],
            send_sem=rsum_ss.at[k],
            recv_sem=rsum_rs.at[who],
            device_id=(who, my_col),
            device_id_type=MESH,
        )

    for k in range(1, rows):
        row_share(k).start()
    store(1).start()
    row_part[my_row] = mine[...]
    for k in range(1, rows):
        row_arrival(k).wait_recv()
    strip_sum = row_part[0]
    for k in range(1, rows):
        strip_sum = strip_sum + row_part[k]
    col_part[my_col] = strip_sum

    def col_share(k, slot):
        return pltpu.make_async_remote_copy(
            src_ref=col_part.at[my_col],
            dst_ref=col_part.at[slot],
            send_sem=csum_ss.at[k],
            recv_sem=csum_rs.at[slot],
            device_id=(my_row, col_peer(k)),
            device_id_type=MESH,
        )

    for k in range(1, cols):
        col_share(k, my_col).start()
    for k in range(1, cols):
        col_share(k, col_peer(k)).wait_recv()
    everything = col_part[0]
    for k in range(1, cols):
        everything = everything + col_part[k]
    everything = jnp.sum(everything, axis=1, keepdims=True)
    moments = [everything[m : m + 1, :] for m in range(2 * ITERS)]
    answer = solve_coefficients(moments)
    result = parts[0]
    for i, scale in enumerate(answer):
        result = result + scale * parts[1 + i]
    results[0] = result
    store(0).start()

    for side in (0, 1):
        @pl.when(has[side])
        def _(side=side):
            for channel in range(CHANNELS):
                row_copy(side, channel).wait_send()
            corner_copy(side).wait_send()

        pl.when(beside[side])(lambda side=side: col_copy(side).wait_send())
    for k in range(1, rows):
        row_share(k).wait_send()
    for i in (0, 1):
        store(i).wait()
    for k in range(1, cols):
        col_share(k, my_col).wait_send()


def local(counts, scatter_vectors, ground_ratio, vertical_wavenumber, initial_phase, initial_extinction):
    high, wide = initial_phase.shape
    rows, cols = counts
    vectors = scatter_vectors.reshape(RAW, high, wide)
    full = wide + LANES
    tall = high + 2 * GHOST
    edges_at = [0]
    for channel in range(CHANNELS):
        held = 4 * REACH + (GUESS * GHOST if channel == 0 else 0)
        edges_at.append(edges_at[-1] + -(-held // 8) * 8)
    edge = edges_at[-1]
    packed = -(-(RAW + GUESS) * SLOT // LANES) * LANES
    f32 = jnp.float32
    dma = pltpu.SemaphoreType.DMA
    out = jax.ShapeDtypeStruct((2, high, wide), f32)
    results = pl.pallas_call(
        functools.partial(kernel, counts, edges_at),
        out_shape=out,
        in_specs=[pl.BlockSpec(memory_space=pltpu.HBM)] * 5,
        out_specs=pl.BlockSpec(memory_space=pltpu.HBM),
        scratch_shapes=[
            pltpu.SMEM((CHANNELS,), f32),
            pltpu.VMEM((RAW, high, wide), f32),
            pltpu.VMEM((high, wide), f32),
            pltpu.VMEM((high, wide), f32),
            pltpu.VMEM((high, wide), f32),
            dma((5,)),
            dma((2,)),
            pltpu.VMEM((2, high, wide), f32),
            pltpu.VMEM((3, tall, full), f32),
            pltpu.VMEM((1 + ITERS, high, wide), f32),
            pltpu.VMEM((5, tall, full), f32),
            pltpu.VMEM((2, edge, wide), f32),
            pltpu.VMEM((2, edge, wide), f32),
            pltpu.VMEM((2, high, packed), f32),
            pltpu.VMEM((2, high, packed), f32),
            pltpu.VMEM((2, 2, SLOT, packed), f32),
            pltpu.VMEM((GUESS, tall, full), f32),
            pltpu.VMEM((RAW, tall, full), f32),
            pltpu.VMEM((tall, full), f32),
            pltpu.VMEM((2, tall, full), f32),
            pltpu.VMEM((8, LANES), f32),
            pltpu.VMEM((rows, 8, LANES), f32),
            pltpu.VMEM((cols, 8, LANES), f32),
            dma((2, CHANNELS)), dma((2, CHANNELS)), dma((2,)), dma((2,)), dma((2,)), dma((2,)),
            dma((rows,)), dma((rows,)), dma((cols,)), dma((cols,)),
        ],
        compiler_params=pltpu.CompilerParams(
            collective_id=0, has_side_effects=True, vmem_limit_bytes=56 * 1024 * 1024
        ),
        cost_estimate=pl.CostEstimate(
            flops=2000 * high * wide, bytes_accessed=80 * high * wide, transcendentals=8 * high * wide
        ),
    )(ground_ratio, vectors, vertical_wavenumber, initial_phase, initial_extinction)
    return (results[0], results[1])


def solution(mesh):
    placed = (
        P(None, None, None, "row", "col"),
        P(),
        P("row", "col"),
        P("row", "col"),
        P("row", "col"),
    )
    counts = (mesh.shape["row"], mesh.shape["col"])
    return jax.shard_map(
        functools.partial(local, counts),
        mesh=mesh,
        in_specs=placed,
        out_specs=(P("row", "col"), P("row", "col")),
        check_vma=False,
    )
```

```python
import functools

import jax
import jax.numpy as jnp
from jax import lax
from jax.experimental import pallas as pl
from jax.experimental.pallas import tpu as pltpu
from jax.sharding import PartitionSpec as P

RADIUS = 9
LAYERS = 16
GAUSS_STEPS = 2
ITERS = 3

EPSILON = 1e-06
DAMPING = 0.002
SMOOTHING = 1.0

CHANNELS = 3
RAW = 4 * CHANNELS
GUESS = 3
GHOST = ITERS + 1
REACH = RADIUS + GHOST
SLOT = 16
LANES = 128
SHIFT = 4.5 * SMOOTHING
MESH = pl.DeviceIdType.MESH


def turn(value, amount, axis):
    size = value.shape[axis]
    amount = amount % size
    return value if amount == 0 else pltpu.roll(value, amount, axis)


def window(value, axis):
    pair = value + turn(value, -1, axis)
    four = pair + turn(pair, -2, axis)
    eight = four + turn(four, -4, axis)
    most = eight + turn(eight, -8, axis)
    return most + turn(pair, -16, axis) + turn(value, -18, axis)


def sine_cosine(angle):
    square = angle * angle
    sine = -1.0 / 39916800.0 + square * (1.0 / 6227020800.0)
    for term in (362880.0, -5040.0, 120.0, -6.0):
        sine = sine * square + 1.0 / term
    sine = angle + angle * square * sine
    cosine = -1.0 / 3628800.0 + square * (1.0 / 479001600.0)
    for term in (40320.0, -720.0, 24.0, -2.0):
        cosine = cosine * square + 1.0 / term
    return sine, 1.0 + square * cosine


def volume_moments(phase, atten):
    sin_half, cos_half = sine_cosine(phase * (0.5 / LAYERS))
    sin_n = 2.0 * sin_half * cos_half
    cos_n = 1.0 - 2.0 * sin_half * sin_half
    grown = jnp.exp(atten * (1.0 / LAYERS))
    weight = 1.0 + grown
    depth = grown
    step_r = grown * cos_n
    step_i = grown * sin_n
    sum_r = 1.0 + step_r
    sum_i = step_i
    deep_r = step_r
    deep_i = step_i
    count = 2
    while count < LAYERS:
        sin_n, cos_n = 2.0 * sin_n * cos_n, 1.0 - 2.0 * sin_n * sin_n
        grown = jnp.exp(atten * (float(count) / LAYERS))
        step_r = grown * cos_n
        step_i = grown * sin_n
        depth = depth + grown * (depth + float(count) * weight)
        weight = weight + grown * weight
        inner_r = deep_r + float(count) * sum_r
        inner_i = deep_i + float(count) * sum_i
        deep_r = deep_r + (step_r * inner_r - step_i * inner_i)
        deep_i = deep_i + (step_r * inner_i + step_i * inner_r)
        sum_r, sum_i = (
            sum_r + (step_r * sum_r - step_i * sum_i),
            sum_i + (step_r * sum_i + step_i * sum_r),
        )
        count *= 2
    scale = 1.0 / weight
    fine = scale * (1.0 / LAYERS)
    deep_r = deep_r + 0.5 * sum_r
    deep_i = deep_i + 0.5 * sum_i
    return (
        depth * fine + 0.5 / LAYERS,
        (cos_half * sum_r - sin_half * sum_i) * scale,
        (cos_half * sum_i + sin_half * sum_r) * scale,
        (cos_half * deep_r - sin_half * deep_i) * fine,
        (cos_half * deep_i + sin_half * deep_r) * fine,
    )


def gauss_newton(phase, atten, known, weighted_re, weighted_im, weight_total, offset_total):
    for step in range(GAUSS_STEPS):
        if step > 0:
            known = volume_moments(phase, atten)
        mean, real, imag, depth_cos, depth_sin = known
        ra = depth_cos - mean * real
        rt = -depth_sin
        ia = depth_sin - mean * imag
        it = depth_cos
        er = weighted_re - weight_total * real - offset_total
        ei = weighted_im - weight_total * imag
        maa = weight_total * (ra * ra + ia * ia) + DAMPING
        map_ = weight_total * (ra * rt + ia * it)
        mpp = weight_total * (rt * rt + it * it) + DAMPING
        ga = ra * er + ia * ei
        gp = rt * er + it * ei
        over = 1.0 / (maa * mpp - map_ * map_)
        atten = atten + (mpp * ga - map_ * gp) * over
        phase = phase + (maa * gp - map_ * ga) * over
    return phase, atten


def dot_poly(left, right, moments):
    total = None
    for i, a in enumerate(left):
        for j, b in enumerate(right):
            term = a * b * moments[i + j]
            total = term if total is None else total + term
    return total


def add_poly(left, right, scale):
    size = max(len(left), len(right))
    out = []
    for i in range(size):
        if i >= len(right):
            out.append(left[i])
        elif i >= len(left):
            out.append(scale * right[i])
        else:
            out.append(left[i] + scale * right[i])
    return out


def solve_coefficients(moments):
    one = jnp.ones_like(moments[0])
    residual = [one]
    direction = [one]
    answer = []
    norm = moments[0]
    for iteration in range(ITERS):
        image = [SHIFT * d for d in direction] + [0.0 * one]
        for i, d in enumerate(direction):
            image[i + 1] = image[i + 1] + d
        step = norm / dot_poly(direction, image, moments)
        answer = add_poly(answer, direction, step)
        if iteration + 1 < ITERS:
            residual = add_poly(residual, image, -step)
            following = dot_poly(residual, residual, moments)
            direction = add_poly(residual, direction, following / norm)
            norm = following
    return answer


def kernel(
    counts, edges_at, ratio_in, vectors_in, wavenumber_in, phase_in, atten_in, parts_out,
    ratio, vectors, wavenumber, phase0, atten0, load_sem, store_sem, results, mixed, parts, first_fit, row_send, row_recv, col_send, col_recv, corner_recv, guess, sums,
    conf_buf, start_buf, mine, row_part, col_part,
    row_ss, row_rs, col_ss, col_rs, corner_ss, corner_rs, rsum_ss, rsum_rs, csum_ss, csum_rs,
):
    rows, cols = counts
    my_row = lax.axis_index("row")
    my_col = lax.axis_index("col")
    high, wide = phase0.shape
    full = wide + LANES
    tall = high + 2 * GHOST
    plain = (wavenumber, phase0, atten0)

    loads = [
        pltpu.make_async_copy(source, target, load_sem.at[i])
        for i, (source, target) in enumerate((
            (vectors_in, vectors), (wavenumber_in, wavenumber),
            (phase_in, phase0), (atten_in, atten0), (ratio_in, ratio),
        ))
    ]
    for load in loads:
        load.start()

    def row_peer(k):
        return lax.rem(my_row + k, rows)

    def col_peer(k):
        return lax.rem(my_col + k, cols)

    barrier = pltpu.get_barrier_semaphore()
    for k in range(1, rows):
        pl.semaphore_signal(barrier, inc=1, device_id=(row_peer(k), my_col), device_id_type=MESH)
    for k in range(1, cols):
        pl.semaphore_signal(barrier, inc=1, device_id=(my_row, col_peer(k)), device_id_type=MESH)

    has = (my_row > 0, my_row < rows - 1)
    beside = (my_col > 0, my_col < cols - 1)

    for side in (0, 1):
        for channel in range(CHANNELS):
            used = edges_at[channel] + 4 * REACH + (GUESS * GHOST if channel == 0 else 0)
            if used < edges_at[channel + 1]:
                spare = edges_at[channel + 1] - used
                row_send[side, used : edges_at[channel + 1], :] = jnp.zeros((spare, wide), jnp.float32)

    lead = (GUESS - 1) * GHOST

    def row_begin(f):
        channel, i = f % CHANNELS, f // CHANNELS
        return edges_at[channel] + (lead if channel == 0 else 0) + i * REACH

    def guess_rows(g):
        begin = g * GHOST if g < GUESS - 1 else lead + 4 * REACH
        return slice(begin, begin + GHOST)

    for load in loads:
        load.wait()
    for g in range(GUESS):
        row_send[0, guess_rows(g), :] = plain[g][0:GHOST, :]
        row_send[1, guess_rows(g), :] = plain[g][high - GHOST : high, :]
    for f in range(RAW):
        span = slice(row_begin(f), row_begin(f) + REACH)
        row_send[0, span, :] = vectors[f, 0:REACH, :]
        row_send[1, span, :] = vectors[f, high - REACH : high, :]

    def row_copy(side, channel):
        span = slice(edges_at[channel], edges_at[channel + 1])
        return pltpu.make_async_remote_copy(
            src_ref=row_send.at[side, span, :],
            dst_ref=row_recv.at[1 - side, span, :],
            send_sem=row_ss.at[side, channel],
            recv_sem=row_rs.at[1 - side, channel],
            device_id=(my_row - 1 + 2 * side, my_col),
            device_id_type=MESH,
        )

    def col_copy(side):
        return pltpu.make_async_remote_copy(
            src_ref=col_send.at[side],
            dst_ref=col_recv.at[1 - side],
            send_sem=col_ss.at[side],
            recv_sem=col_rs.at[1 - side],
            device_id=(my_row, my_col - 1 + 2 * side),
            device_id_type=MESH,
        )

    def corner_copy(side):
        begin = 0 if side == 0 else high - SLOT
        return pltpu.make_async_remote_copy(
            src_ref=col_recv.at[:, begin : begin + SLOT, :],
            dst_ref=corner_recv.at[1 - side],
            send_sem=corner_ss.at[side],
            recv_sem=corner_rs.at[1 - side],
            device_id=(my_row - 1 + 2 * side, my_col),
            device_id_type=MESH,
        )

    pl.semaphore_wait(barrier, rows + cols - 2)
    for channel in range(CHANNELS - 1):
        for side in (0, 1):
            pl.when(has[side])(lambda side=side, channel=channel: row_copy(side, channel).start())

    lane = lax.broadcasted_iota(jnp.int32, (high, LANES), 1)
    per = LANES // SLOT
    packs = (RAW + GUESS + per - 1) // per
    for k in range(packs):
        low = jnp.zeros((high, LANES), jnp.float32)
        top = jnp.zeros((high, LANES), jnp.float32)
        for p in range(per):
            f = k * per + p
            if f >= RAW + GUESS:
                continue
            if f < RAW:
                first, last = vectors[f, :, 0:LANES], vectors[f, :, wide - LANES : wide]
            else:
                ref = plain[f - RAW]
                first, last = ref[:, 0:LANES], ref[:, wide - LANES : wide]
            here = (lane >= p * SLOT) & (lane < (p + 1) * SLOT)
            low = jnp.where(here, turn(first, p * SLOT, 1), low)
            top = jnp.where(here, turn(last, (p + 1) * SLOT, 1), top)
        col_send[0, :, k * LANES : (k + 1) * LANES] = low
        col_send[1, :, k * LANES : (k + 1) * LANES] = top

    for side in (0, 1):
        pl.when(beside[side])(lambda side=side: col_copy(side).start())

    for side in (0, 1):
        @pl.when(jnp.logical_not(has[side]))
        def _(side=side):
            row_recv[side] = jnp.zeros(row_recv.shape[1:], jnp.float32)
            corner_recv[side] = jnp.zeros(corner_recv.shape[1:], jnp.float32)

        @pl.when(jnp.logical_not(beside[side]))
        def _(side=side):
            col_recv[side] = jnp.zeros(col_recv.shape[1:], jnp.float32)

    def products(raws):
        re1, im1, re2, im2 = raws
        return (
            re1 * re1 + im1 * im1,
            re2 * re2 + im2 * im2,
            re1 * re2 + im1 * im2,
            re1 * im2 - im1 * re2,
        )

    deep = -(-(2 * REACH + high) // 8) * 8
    above_own = jnp.zeros((REACH, LANES), jnp.float32)
    below_own = jnp.zeros((deep - REACH - high, LANES), jnp.float32)

    def own_sums(channel, raws, piece):
        for i, product in enumerate(products(raws)):
            placed = jnp.concatenate([above_own, product, below_own], axis=0)
            sums[4 * channel + i, :, piece] = window(placed, 0)[0:tall, :]

    def inner_sums(channel, carry):
        for strip in range(wide // LANES):
            piece = slice(strip * LANES, (strip + 1) * LANES)
            own_sums(channel, [vectors[CHANNELS * i + channel, :, piece] for i in range(4)], piece)
        return carry

    lax.fori_loop(0, CHANNELS, inner_sums, 0)
    for g in range(GUESS):
        guess[g, GHOST : GHOST + high, 0:wide] = plain[g][...]

    for side in (0, 1):
        pl.when(beside[side])(lambda side=side: col_copy(1 - side).wait_recv())
    for side in (0, 1):
        pl.when(has[side])(lambda side=side: corner_copy(side).start())
    for side in (0, 1):
        pl.when(has[side])(lambda side=side: row_copy(side, CHANNELS - 1).start())

    def unpacked(left, right, f):
        p = f % per
        place = lax.broadcasted_iota(jnp.int32, left.shape, 1)
        return jnp.where(
            place < LANES // 2,
            turn(right, -p * SLOT, 1),
            turn(left, LANES - SLOT - p * SLOT, 1),
        )

    def outer(f):
        piece = slice(f // per * LANES, (f // per + 1) * LANES)
        return unpacked(col_recv[0, :, piece], col_recv[1, :, piece], f)

    for channel in range(CHANNELS):
        own_sums(channel, [outer(CHANNELS * i + channel) for i in range(4)], slice(wide, full))
    for g in range(GUESS):
        guess[g, GHOST : GHOST + high, wide:full] = outer(RAW + g)

    ratios = [jnp.full((1, full), ratio[k], jnp.float32) for k in range(CHANNELS)]
    weights = [1.0 / (1.0 + r) for r in ratios]
    weight_total = sum(w * w for w in weights)
    offset_total = sum(r * w * w for r, w in zip(ratios, weights))

    def cohere(channel, chunk):
        block = pl.ds(pl.multiple_of(chunk * 8, 8), 8)
        power1, power2, cross_re, cross_im = [
            window(sums[4 * channel + i, block, :], 1) for i in range(4)
        ]
        scale = lax.rsqrt(power1 * power2 + EPSILON)
        real = cross_re * scale
        imag = cross_im * scale
        found = (real * weights[channel], imag * weights[channel], real * real + imag * imag)
        for i, value in enumerate(found):
            if channel == 0:
                mixed[i, block, :] = value
            else:
                mixed[i, block, :] += value

    def fit(chunk):
        block = pl.ds(pl.multiple_of(chunk * 8, 8), 8)
        weighted_re, weighted_im, confidence = [turn(mixed[i, block, :], RADIUS, 1) for i in range(3)]
        phase, atten = gauss_newton(
            guess[1, block, :], guess[2, block, :], [first_fit[i, block, :] for i in range(5)],
            weighted_re, weighted_im, weight_total, offset_total,
        )
        conf_buf[block, :] = confidence * (1.0 / CHANNELS)
        start_buf[0, block, :] = phase / guess[0, block, :]
        start_buf[1, block, :] = atten

    for g in range(GUESS):
        guess[g, 0:GHOST, :] = jnp.zeros((GHOST, full), jnp.float32)
        guess[g, GHOST + high : tall, :] = jnp.zeros((GHOST, full), jnp.float32)

    def guessed(chunk, carry):
        block = pl.ds(pl.multiple_of(chunk * 8, 8), 8)
        for i, moment in enumerate(volume_moments(guess[1, block, :], guess[2, block, :])):
            first_fit[i, block, :] = moment
        return carry

    chunks = tall // 8
    edge_chunks = SLOT // 8

    def middle(chunk, carry):
        for channel in range(CHANNELS):
            cohere(channel, chunk)
        fit(chunk)
        return carry

    lax.fori_loop(0, chunks, guessed, 0)
    lax.fori_loop(edge_chunks, chunks - edge_chunks, middle, 0)

    line = lax.broadcasted_iota(jnp.int32, (SLOT, LANES), 0)
    keep = (line < REACH, line >= SLOT - REACH)

    def running(value, down):
        for k in (1, 2, 4, 8):
            if down:
                value = value + jnp.where(line >= k, turn(value, k, 0), 0.0)
            else:
                value = value + jnp.where(line < SLOT - k, turn(value, -k, 0), 0.0)
        return value

    def corner(side, f):
        piece = slice(f // per * LANES, (f // per + 1) * LANES)
        return unpacked(corner_recv[side, 0, :, piece], corner_recv[side, 1, :, piece], f)

    def halo_rows(side, f, strip):
        if strip < wide // LANES:
            begin = row_begin(f) - side * (SLOT - REACH)
            value = row_recv[side, begin : begin + SLOT, strip * LANES : (strip + 1) * LANES]
        else:
            value = turn(corner(side, f), (1 - 2 * side) * (REACH - SLOT), 0)
        return jnp.where(keep[side], value, 0.0)

    def edge_chunk(step):
        return step + step // edge_chunks * (chunks - 2 * edge_chunks)

    for channel in range(CHANNELS):
        for side in (0, 1):
            @pl.when(has[side])
            def _(side=side, channel=channel):
                row_copy(1 - side, channel).wait_recv()
                if channel == 0:
                    corner_copy(1 - side).wait_recv()

        for side in (0, 1):
            begin = side * (tall - SLOT)
            for strip in range(full // LANES):
                piece = slice(strip * LANES, (strip + 1) * LANES)
                raws = [halo_rows(side, CHANNELS * i + channel, strip) for i in range(4)]
                for i, product in enumerate(products(raws)):
                    sums[4 * channel + i, begin : begin + SLOT, piece] += running(product, side == 1)

        def edge_cohere(step, carry, channel=channel):
            cohere(channel, edge_chunk(step))
            return carry

        lax.fori_loop(0, 2 * edge_chunks, edge_cohere, 0)
        if channel == 0:
            for g in range(GUESS):
                span = guess_rows(g)
                guess[g, 0:GHOST, 0:wide] = row_recv[0, span, :]
                guess[g, GHOST + high : tall, 0:wide] = row_recv[1, span, :]
                guess[g, 0:GHOST, wide:full] = corner(0, RAW + g)[SLOT - GHOST :, :]
                guess[g, GHOST + high : tall, wide:full] = corner(1, RAW + g)[0:GHOST, :]

            ghosts = [
                jnp.concatenate([guess[g, 0:GHOST, :], guess[g, GHOST + high : tall, :]], axis=0) for g in (1, 2)
            ]
            for i, moment in enumerate(volume_moments(*ghosts)):
                first_fit[i, 0:GHOST, :] = moment[0:GHOST, :]
                first_fit[i, GHOST + high : tall, :] = moment[GHOST : 2 * GHOST, :]

    def edges(step, carry):
        fit(edge_chunk(step))
        return carry

    lax.fori_loop(0, 2 * edge_chunks, edges, 0, unroll=2)

    row_at = lax.broadcasted_iota(jnp.int32, (tall, full), 0) - GHOST
    lane_at = lax.broadcasted_iota(jnp.int32, (tall, full), 1)
    col_at = jnp.where(lane_at < wide + LANES // 2, lane_at, lane_at - full)
    near = (col_at >= -GHOST) & (col_at < wide + GHOST)
    row_all = row_at + my_row * high
    col_all = col_at + my_col * wide
    inside = near & (row_all >= 0) & (row_all < rows * high) & (col_all >= 0) & (col_all < cols * wide)

    def masked(value):
        return jnp.where(inside, value, 0.0)

    def around(value):
        return turn(value, 1, 0) + turn(value, -1, 0) + turn(value, 1, 1) + turn(value, -1, 1)

    start = masked(start_buf[0])
    confidence = conf_buf[...]
    centred = confidence + (4.0 * SMOOTHING - SHIFT)
    basis = [masked(SMOOTHING * (around(start) - 4.0 * start))]
    for _ in range(ITERS - 1):
        basis.append(masked(centred * basis[-1] - SMOOTHING * around(basis[-1])))
    basis.append(centred * basis[-1] - SMOOTHING * around(basis[-1]))

    parts[0] = start[GHOST : GHOST + high, 0:wide]
    for i in range(ITERS):
        parts[1 + i] = basis[i][GHOST : GHOST + high, 0:wide]
    results[1] = start_buf[1, GHOST : GHOST + high, 0:wide]

    def store(i):
        return pltpu.make_async_copy(results.at[i], parts_out.at[i], store_sem.at[i])

    own = inside & (row_at >= 0) & (row_at < high) & (lane_at < wide)
    for m in range(2 * ITERS):
        product = jnp.where(own, basis[m // 2] * basis[m - m // 2], 0.0)
        line = jnp.sum(product, axis=0, keepdims=True)
        total = line[:, 0:LANES]
        for strip in range(1, wide // LANES):
            total = total + line[:, strip * LANES : (strip + 1) * LANES]
        mine[m : m + 1, :] = total
    mine[2 * ITERS :, :] = jnp.zeros((8 - 2 * ITERS, LANES), jnp.float32)

    def row_share(k):
        return pltpu.make_async_remote_copy(
            src_ref=mine,
            dst_ref=row_part.at[my_row],
            send_sem=rsum_ss.at[k],
            recv_sem=rsum_rs.at[my_row],
            device_id=(row_peer(k), my_col),
            device_id_type=MESH,
        )

    def row_arrival(k):
        who = row_peer(k)
        return pltpu.make_async_remote_copy(
            src_ref=mine,
            dst_ref=row_part.at[who],
            send_sem=rsum_ss.at[k],
            recv_sem=rsum_rs.at[who],
            device_id=(who, my_col),
            device_id_type=MESH,
        )

    for k in range(1, rows):
        row_share(k).start()
    store(1).start()
    row_part[my_row] = mine[...]
    for k in range(1, rows):
        row_arrival(k).wait_recv()
    strip_sum = row_part[0]
    for k in range(1, rows):
        strip_sum = strip_sum + row_part[k]
    col_part[my_col] = strip_sum

    def col_share(k, slot):
        return pltpu.make_async_remote_copy(
            src_ref=col_part.at[my_col],
            dst_ref=col_part.at[slot],
            send_sem=csum_ss.at[k],
            recv_sem=csum_rs.at[slot],
            device_id=(my_row, col_peer(k)),
            device_id_type=MESH,
        )

    for k in range(1, cols):
        col_share(k, my_col).start()
    for k in range(1, cols):
        col_share(k, col_peer(k)).wait_recv()
    everything = col_part[0]
    for k in range(1, cols):
        everything = everything + col_part[k]
    everything = jnp.sum(everything, axis=1, keepdims=True)
    moments = [everything[m : m + 1, :] for m in range(2 * ITERS)]
    answer = solve_coefficients(moments)
    result = parts[0]
    for i, scale in enumerate(answer):
        result = result + scale * parts[1 + i]
    results[0] = result
    store(0).start()

    for side in (0, 1):
        @pl.when(has[side])
        def _(side=side):
            for channel in range(CHANNELS):
                row_copy(side, channel).wait_send()
            corner_copy(side).wait_send()

        pl.when(beside[side])(lambda side=side: col_copy(side).wait_send())
    for k in range(1, rows):
        row_share(k).wait_send()
    for i in (0, 1):
        store(i).wait()
    for k in range(1, cols):
        col_share(k, my_col).wait_send()


def local(counts, scatter_vectors, ground_ratio, vertical_wavenumber, initial_phase, initial_extinction):
    high, wide = initial_phase.shape
    rows, cols = counts
    vectors = scatter_vectors.reshape(RAW, high, wide)
    full = wide + LANES
    tall = high + 2 * GHOST
    edges_at = [0]
    for channel in range(CHANNELS):
        held = 4 * REACH + (GUESS * GHOST if channel == 0 else 0)
        edges_at.append(edges_at[-1] + -(-held // 8) * 8)
    edge = edges_at[-1]
    packed = -(-(RAW + GUESS) * SLOT // LANES) * LANES
    f32 = jnp.float32
    dma = pltpu.SemaphoreType.DMA
    out = jax.ShapeDtypeStruct((2, high, wide), f32)
    results = pl.pallas_call(
        functools.partial(kernel, counts, edges_at),
        out_shape=out,
        in_specs=[pl.BlockSpec(memory_space=pltpu.HBM)] * 5,
        out_specs=pl.BlockSpec(memory_space=pltpu.HBM),
        scratch_shapes=[
            pltpu.SMEM((CHANNELS,), f32),
            pltpu.VMEM((RAW, high, wide), f32),
            pltpu.VMEM((high, wide), f32),
            pltpu.VMEM((high, wide), f32),
            pltpu.VMEM((high, wide), f32),
            dma((5,)),
            dma((2,)),
            pltpu.VMEM((2, high, wide), f32),
            pltpu.VMEM((3, tall, full), f32),
            pltpu.VMEM((1 + ITERS, high, wide), f32),
            pltpu.VMEM((5, tall, full), f32),
            pltpu.VMEM((2, edge, wide), f32),
            pltpu.VMEM((2, edge, wide), f32),
            pltpu.VMEM((2, high, packed), f32),
            pltpu.VMEM((2, high, packed), f32),
            pltpu.VMEM((2, 2, SLOT, packed), f32),
            pltpu.VMEM((GUESS, tall, full), f32),
            pltpu.VMEM((RAW, tall, full), f32),
            pltpu.VMEM((tall, full), f32),
            pltpu.VMEM((2, tall, full), f32),
            pltpu.VMEM((8, LANES), f32),
            pltpu.VMEM((rows, 8, LANES), f32),
            pltpu.VMEM((cols, 8, LANES), f32),
            dma((2, CHANNELS)), dma((2, CHANNELS)), dma((2,)), dma((2,)), dma((2,)), dma((2,)),
            dma((rows,)), dma((rows,)), dma((cols,)), dma((cols,)),
        ],
        compiler_params=pltpu.CompilerParams(
            collective_id=0, has_side_effects=True, vmem_limit_bytes=56 * 1024 * 1024
        ),
        cost_estimate=pl.CostEstimate(
            flops=2000 * high * wide, bytes_accessed=80 * high * wide, transcendentals=8 * high * wide
        ),
    )(ground_ratio, vectors, vertical_wavenumber, initial_phase, initial_extinction)
    return (results[0], results[1])


def solution(mesh):
    placed = (
        P(None, None, None, "row", "col"),
        P(),
        P("row", "col"),
        P("row", "col"),
        P("row", "col"),
    )
    counts = (mesh.shape["row"], mesh.shape["col"])
    return jax.shard_map(
        functools.partial(local, counts),
        mesh=mesh,
        in_specs=placed,
        out_specs=(P("row", "col"), P("row", "col")),
        check_vma=False,
    )
```

```python
import functools

import jax
import jax.numpy as jnp
from jax import lax
from jax.experimental import pallas as pl
from jax.experimental.pallas import tpu as pltpu
from jax.sharding import PartitionSpec as P

RADIUS = 9
LAYERS = 16
GAUSS_STEPS = 2
ITERS = 3

EPSILON = 1e-06
DAMPING = 0.002
SMOOTHING = 1.0

CHANNELS = 3
RAW = 4 * CHANNELS
GUESS = 3
GHOST = ITERS + 1
REACH = RADIUS + GHOST
SLOT = 16
LANES = 128
SHIFT = 4.5 * SMOOTHING
MESH = pl.DeviceIdType.MESH


def turn(value, amount, axis):
    size = value.shape[axis]
    amount = amount % size
    return value if amount == 0 else pltpu.roll(value, amount, axis)


def window(value, axis):
    pair = value + turn(value, -1, axis)
    four = pair + turn(pair, -2, axis)
    eight = four + turn(four, -4, axis)
    most = eight + turn(eight, -8, axis)
    return most + turn(pair, -16, axis) + turn(value, -18, axis)


def sine_cosine(angle):
    square = angle * angle
    sine = -1.0 / 39916800.0 + square * (1.0 / 6227020800.0)
    for term in (362880.0, -5040.0, 120.0, -6.0):
        sine = sine * square + 1.0 / term
    sine = angle + angle * square * sine
    cosine = -1.0 / 3628800.0 + square * (1.0 / 479001600.0)
    for term in (40320.0, -720.0, 24.0, -2.0):
        cosine = cosine * square + 1.0 / term
    return sine, 1.0 + square * cosine


def volume_moments(phase, atten):
    sin_half, cos_half = sine_cosine(phase * (0.5 / LAYERS))
    sin_n = 2.0 * sin_half * cos_half
    cos_n = 1.0 - 2.0 * sin_half * sin_half
    grown = jnp.exp(atten * (1.0 / LAYERS))
    weight = 1.0 + grown
    depth = grown
    step_r = grown * cos_n
    step_i = grown * sin_n
    sum_r = 1.0 + step_r
    sum_i = step_i
    deep_r = step_r
    deep_i = step_i
    count = 2
    while count < LAYERS:
        sin_n, cos_n = 2.0 * sin_n * cos_n, 1.0 - 2.0 * sin_n * sin_n
        grown = jnp.exp(atten * (float(count) / LAYERS))
        step_r = grown * cos_n
        step_i = grown * sin_n
        depth = depth + grown * (depth + float(count) * weight)
        weight = weight + grown * weight
        inner_r = deep_r + float(count) * sum_r
        inner_i = deep_i + float(count) * sum_i
        deep_r = deep_r + (step_r * inner_r - step_i * inner_i)
        deep_i = deep_i + (step_r * inner_i + step_i * inner_r)
        sum_r, sum_i = (
            sum_r + (step_r * sum_r - step_i * sum_i),
            sum_i + (step_r * sum_i + step_i * sum_r),
        )
        count *= 2
    scale = 1.0 / weight
    fine = scale * (1.0 / LAYERS)
    deep_r = deep_r + 0.5 * sum_r
    deep_i = deep_i + 0.5 * sum_i
    return (
        depth * fine + 0.5 / LAYERS,
        (cos_half * sum_r - sin_half * sum_i) * scale,
        (cos_half * sum_i + sin_half * sum_r) * scale,
        (cos_half * deep_r - sin_half * deep_i) * fine,
        (cos_half * deep_i + sin_half * deep_r) * fine,
    )


def gauss_newton(phase, atten, known, weighted_re, weighted_im, weight_total, offset_total):
    for step in range(GAUSS_STEPS):
        if step > 0:
            known = volume_moments(phase, atten)
        mean, real, imag, depth_cos, depth_sin = known
        ra = depth_cos - mean * real
        rt = -depth_sin
        ia = depth_sin - mean * imag
        it = depth_cos
        er = weighted_re - weight_total * real - offset_total
        ei = weighted_im - weight_total * imag
        maa = weight_total * (ra * ra + ia * ia) + DAMPING
        map_ = weight_total * (ra * rt + ia * it)
        mpp = weight_total * (rt * rt + it * it) + DAMPING
        ga = ra * er + ia * ei
        gp = rt * er + it * ei
        over = 1.0 / (maa * mpp - map_ * map_)
        atten = atten + (mpp * ga - map_ * gp) * over
        phase = phase + (maa * gp - map_ * ga) * over
    return phase, atten


def dot_poly(left, right, moments):
    total = None
    for i, a in enumerate(left):
        for j, b in enumerate(right):
            term = a * b * moments[i + j]
            total = term if total is None else total + term
    return total


def add_poly(left, right, scale):
    size = max(len(left), len(right))
    out = []
    for i in range(size):
        if i >= len(right):
            out.append(left[i])
        elif i >= len(left):
            out.append(scale * right[i])
        else:
            out.append(left[i] + scale * right[i])
    return out


def solve_coefficients(moments):
    one = jnp.ones_like(moments[0])
    residual = [one]
    direction = [one]
    answer = []
    norm = moments[0]
    for iteration in range(ITERS):
        image = [SHIFT * d for d in direction] + [0.0 * one]
        for i, d in enumerate(direction):
            image[i + 1] = image[i + 1] + d
        step = norm / dot_poly(direction, image, moments)
        answer = add_poly(answer, direction, step)
        if iteration + 1 < ITERS:
            residual = add_poly(residual, image, -step)
            following = dot_poly(residual, residual, moments)
            direction = add_poly(residual, direction, following / norm)
            norm = following
    return answer


def kernel(
    counts, edges_at, ratio_in, vectors_in, wavenumber_in, phase_in, atten_in, parts_out,
    ratio, vectors, wavenumber, phase0, atten0, load_sem, store_sem, results, mixed, parts, first_fit, row_send, row_recv, col_send, col_recv, corner_recv, guess, sums,
    conf_buf, start_buf, mine, row_part, col_part,
    row_ss, row_rs, col_ss, col_rs, corner_ss, corner_rs, rsum_ss, rsum_rs, csum_ss, csum_rs,
):
    rows, cols = counts
    my_row = lax.axis_index("row")
    my_col = lax.axis_index("col")
    high, wide = phase0.shape
    full = wide + LANES
    tall = high + 2 * GHOST
    plain = (wavenumber, phase0, atten0)

    loads = [
        pltpu.make_async_copy(source, target, load_sem.at[i])
        for i, (source, target) in enumerate((
            (vectors_in, vectors), (wavenumber_in, wavenumber),
            (phase_in, phase0), (atten_in, atten0), (ratio_in, ratio),
        ))
    ]
    for load in loads:
        load.start()

    def row_peer(k):
        return lax.rem(my_row + k, rows)

    def col_peer(k):
        return lax.rem(my_col + k, cols)

    barrier = pltpu.get_barrier_semaphore()
    for k in range(1, rows):
        pl.semaphore_signal(barrier, inc=1, device_id=(row_peer(k), my_col), device_id_type=MESH)
    for k in range(1, cols):
        pl.semaphore_signal(barrier, inc=1, device_id=(my_row, col_peer(k)), device_id_type=MESH)

    has = (my_row > 0, my_row < rows - 1)
    beside = (my_col > 0, my_col < cols - 1)

    for side in (0, 1):
        for channel in range(CHANNELS):
            used = edges_at[channel] + 4 * REACH + (GUESS * GHOST if channel == 0 else 0)
            if used < edges_at[channel + 1]:
                spare = edges_at[channel + 1] - used
                row_send[side, used : edges_at[channel + 1], :] = jnp.zeros((spare, wide), jnp.float32)

    lead = (GUESS - 1) * GHOST

    def row_begin(f):
        channel, i = f % CHANNELS, f // CHANNELS
        return edges_at[channel] + (lead if channel == 0 else 0) + i * REACH

    def guess_rows(g):
        begin = g * GHOST if g < GUESS - 1 else lead + 4 * REACH
        return slice(begin, begin + GHOST)

    for load in loads:
        load.wait()
    for g in range(GUESS):
        row_send[0, guess_rows(g), :] = plain[g][0:GHOST, :]
        row_send[1, guess_rows(g), :] = plain[g][high - GHOST : high, :]
    for f in range(RAW):
        span = slice(row_begin(f), row_begin(f) + REACH)
        row_send[0, span, :] = vectors[f, 0:REACH, :]
        row_send[1, span, :] = vectors[f, high - REACH : high, :]

    def row_copy(side, channel):
        span = slice(edges_at[channel], edges_at[channel + 1])
        return pltpu.make_async_remote_copy(
            src_ref=row_send.at[side, span, :],
            dst_ref=row_recv.at[1 - side, span, :],
            send_sem=row_ss.at[side, channel],
            recv_sem=row_rs.at[1 - side, channel],
            device_id=(my_row - 1 + 2 * side, my_col),
            device_id_type=MESH,
        )

    def col_copy(side):
        return pltpu.make_async_remote_copy(
            src_ref=col_send.at[side],
            dst_ref=col_recv.at[1 - side],
            send_sem=col_ss.at[side],
            recv_sem=col_rs.at[1 - side],
            device_id=(my_row, my_col - 1 + 2 * side),
            device_id_type=MESH,
        )

    def corner_copy(side):
        begin = 0 if side == 0 else high - SLOT
        return pltpu.make_async_remote_copy(
            src_ref=col_recv.at[:, begin : begin + SLOT, :],
            dst_ref=corner_recv.at[1 - side],
            send_sem=corner_ss.at[side],
            recv_sem=corner_rs.at[1 - side],
            device_id=(my_row - 1 + 2 * side, my_col),
            device_id_type=MESH,
        )

    lane = lax.broadcasted_iota(jnp.int32, (high, LANES), 1)
    per = LANES // SLOT
    packs = (RAW + GUESS + per - 1) // per
    for k in range(packs):
        low = jnp.zeros((high, LANES), jnp.float32)
        top = jnp.zeros((high, LANES), jnp.float32)
        for p in range(per):
            f = k * per + p
            if f >= RAW + GUESS:
                continue
            if f < RAW:
                first, last = vectors[f, :, 0:LANES], vectors[f, :, wide - LANES : wide]
            else:
                ref = plain[f - RAW]
                first, last = ref[:, 0:LANES], ref[:, wide - LANES : wide]
            here = (lane >= p * SLOT) & (lane < (p + 1) * SLOT)
            low = jnp.where(here, turn(first, p * SLOT, 1), low)
            top = jnp.where(here, turn(last, (p + 1) * SLOT, 1), top)
        col_send[0, :, k * LANES : (k + 1) * LANES] = low
        col_send[1, :, k * LANES : (k + 1) * LANES] = top

    pl.semaphore_wait(barrier, rows + cols - 2)
    for side in (0, 1):
        pl.when(beside[side])(lambda side=side: col_copy(side).start())
    for channel in range(CHANNELS - 1):
        for side in (0, 1):
            pl.when(has[side])(lambda side=side, channel=channel: row_copy(side, channel).start())


    for side in (0, 1):
        @pl.when(jnp.logical_not(has[side]))
        def _(side=side):
            row_recv[side] = jnp.zeros(row_recv.shape[1:], jnp.float32)
            corner_recv[side] = jnp.zeros(corner_recv.shape[1:], jnp.float32)

        @pl.when(jnp.logical_not(beside[side]))
        def _(side=side):
            col_recv[side] = jnp.zeros(col_recv.shape[1:], jnp.float32)

    def products(raws):
        re1, im1, re2, im2 = raws
        return (
            re1 * re1 + im1 * im1,
            re2 * re2 + im2 * im2,
            re1 * re2 + im1 * im2,
            re1 * im2 - im1 * re2,
        )

    deep = -(-(2 * REACH + high) // 8) * 8
    above_own = jnp.zeros((REACH, LANES), jnp.float32)
    below_own = jnp.zeros((deep - REACH - high, LANES), jnp.float32)

    def own_sums(channel, raws, piece):
        for i, product in enumerate(products(raws)):
            placed = jnp.concatenate([above_own, product, below_own], axis=0)
            sums[4 * channel + i, :, piece] = window(placed, 0)[0:tall, :]

    def inner_sums(channel, carry):
        for strip in range(wide // LANES):
            piece = slice(strip * LANES, (strip + 1) * LANES)
            own_sums(channel, [vectors[CHANNELS * i + channel, :, piece] for i in range(4)], piece)
        return carry

    lax.fori_loop(0, CHANNELS, inner_sums, 0)
    for g in range(GUESS):
        guess[g, GHOST : GHOST + high, 0:wide] = plain[g][...]

    for side in (0, 1):
        pl.when(beside[side])(lambda side=side: col_copy(1 - side).wait_recv())
    for side in (0, 1):
        pl.when(has[side])(lambda side=side: corner_copy(side).start())
    for side in (0, 1):
        pl.when(has[side])(lambda side=side: row_copy(side, CHANNELS - 1).start())

    def unpacked(left, right, f):
        p = f % per
        place = lax.broadcasted_iota(jnp.int32, left.shape, 1)
        return jnp.where(
            place < LANES // 2,
            turn(right, -p * SLOT, 1),
            turn(left, LANES - SLOT - p * SLOT, 1),
        )

    def outer(f):
        piece = slice(f // per * LANES, (f // per + 1) * LANES)
        return unpacked(col_recv[0, :, piece], col_recv[1, :, piece], f)

    for channel in range(CHANNELS):
        own_sums(channel, [outer(CHANNELS * i + channel) for i in range(4)], slice(wide, full))
    for g in range(GUESS):
        guess[g, GHOST : GHOST + high, wide:full] = outer(RAW + g)

    ratios = [jnp.full((1, full), ratio[k], jnp.float32) for k in range(CHANNELS)]
    weights = [1.0 / (1.0 + r) for r in ratios]
    weight_total = sum(w * w for w in weights)
    offset_total = sum(r * w * w for r, w in zip(ratios, weights))

    def cohere(channel, chunk):
        block = pl.ds(pl.multiple_of(chunk * 8, 8), 8)
        power1, power2, cross_re, cross_im = [
            window(sums[4 * channel + i, block, :], 1) for i in range(4)
        ]
        scale = lax.rsqrt(power1 * power2 + EPSILON)
        real = cross_re * scale
        imag = cross_im * scale
        found = (real * weights[channel], imag * weights[channel], real * real + imag * imag)
        for i, value in enumerate(found):
            if channel == 0:
                mixed[i, block, :] = value
            else:
                mixed[i, block, :] += value

    def fit(chunk):
        block = pl.ds(pl.multiple_of(chunk * 8, 8), 8)
        weighted_re, weighted_im, confidence = [turn(mixed[i, block, :], RADIUS, 1) for i in range(3)]
        phase, atten = gauss_newton(
            guess[1, block, :], guess[2, block, :], [first_fit[i, block, :] for i in range(5)],
            weighted_re, weighted_im, weight_total, offset_total,
        )
        conf_buf[block, :] = confidence * (1.0 / CHANNELS)
        start_buf[0, block, :] = phase / guess[0, block, :]
        start_buf[1, block, :] = atten

    for g in range(GUESS):
        guess[g, 0:GHOST, :] = jnp.zeros((GHOST, full), jnp.float32)
        guess[g, GHOST + high : tall, :] = jnp.zeros((GHOST, full), jnp.float32)

    def guessed(chunk, carry):
        block = pl.ds(pl.multiple_of(chunk * 8, 8), 8)
        for i, moment in enumerate(volume_moments(guess[1, block, :], guess[2, block, :])):
            first_fit[i, block, :] = moment
        return carry

    chunks = tall // 8
    edge_chunks = SLOT // 8

    def middle(chunk, carry):
        for channel in range(CHANNELS):
            cohere(channel, chunk)
        fit(chunk)
        return carry

    lax.fori_loop(0, chunks, guessed, 0)
    lax.fori_loop(edge_chunks, chunks - edge_chunks, middle, 0)

    line = lax.broadcasted_iota(jnp.int32, (SLOT, LANES), 0)
    keep = (line < REACH, line >= SLOT - REACH)

    def running(value, down):
        for k in (1, 2, 4, 8):
            if down:
                value = value + jnp.where(line >= k, turn(value, k, 0), 0.0)
            else:
                value = value + jnp.where(line < SLOT - k, turn(value, -k, 0), 0.0)
        return value

    def corner(side, f):
        piece = slice(f // per * LANES, (f // per + 1) * LANES)
        return unpacked(corner_recv[side, 0, :, piece], corner_recv[side, 1, :, piece], f)

    def halo_rows(side, f, strip):
        if strip < wide // LANES:
            begin = row_begin(f) - side * (SLOT - REACH)
            value = row_recv[side, begin : begin + SLOT, strip * LANES : (strip + 1) * LANES]
        else:
            value = turn(corner(side, f), (1 - 2 * side) * (REACH - SLOT), 0)
        return jnp.where(keep[side], value, 0.0)

    def edge_chunk(step):
        return step + step // edge_chunks * (chunks - 2 * edge_chunks)

    for channel in range(CHANNELS):
        for side in (0, 1):
            @pl.when(has[side])
            def _(side=side, channel=channel):
                row_copy(1 - side, channel).wait_recv()
                if channel == 0:
                    corner_copy(1 - side).wait_recv()

        for side in (0, 1):
            begin = side * (tall - SLOT)
            for strip in range(full // LANES):
                piece = slice(strip * LANES, (strip + 1) * LANES)
                raws = [halo_rows(side, CHANNELS * i + channel, strip) for i in range(4)]
                for i, product in enumerate(products(raws)):
                    sums[4 * channel + i, begin : begin + SLOT, piece] += running(product, side == 1)

        def edge_cohere(step, carry, channel=channel):
            cohere(channel, edge_chunk(step))
            return carry

        lax.fori_loop(0, 2 * edge_chunks, edge_cohere, 0)
        if channel == 0:
            for g in range(GUESS):
                span = guess_rows(g)
                guess[g, 0:GHOST, 0:wide] = row_recv[0, span, :]
                guess[g, GHOST + high : tall, 0:wide] = row_recv[1, span, :]
                guess[g, 0:GHOST, wide:full] = corner(0, RAW + g)[SLOT - GHOST :, :]
                guess[g, GHOST + high : tall, wide:full] = corner(1, RAW + g)[0:GHOST, :]

            ghosts = [
                jnp.concatenate([guess[g, 0:GHOST, :], guess[g, GHOST + high : tall, :]], axis=0) for g in (1, 2)
            ]
            for i, moment in enumerate(volume_moments(*ghosts)):
                first_fit[i, 0:GHOST, :] = moment[0:GHOST, :]
                first_fit[i, GHOST + high : tall, :] = moment[GHOST : 2 * GHOST, :]

    def edges(step, carry):
        fit(edge_chunk(step))
        return carry

    lax.fori_loop(0, 2 * edge_chunks, edges, 0, unroll=2)

    row_at = lax.broadcasted_iota(jnp.int32, (tall, full), 0) - GHOST
    lane_at = lax.broadcasted_iota(jnp.int32, (tall, full), 1)
    col_at = jnp.where(lane_at < wide + LANES // 2, lane_at, lane_at - full)
    near = (col_at >= -GHOST) & (col_at < wide + GHOST)
    row_all = row_at + my_row * high
    col_all = col_at + my_col * wide
    inside = near & (row_all >= 0) & (row_all < rows * high) & (col_all >= 0) & (col_all < cols * wide)

    def masked(value):
        return jnp.where(inside, value, 0.0)

    def around(value):
        return turn(value, 1, 0) + turn(value, -1, 0) + turn(value, 1, 1) + turn(value, -1, 1)

    start = masked(start_buf[0])
    confidence = conf_buf[...]
    centred = confidence + (4.0 * SMOOTHING - SHIFT)
    basis = [masked(SMOOTHING * (around(start) - 4.0 * start))]
    for _ in range(ITERS - 1):
        basis.append(masked(centred * basis[-1] - SMOOTHING * around(basis[-1])))
    basis.append(centred * basis[-1] - SMOOTHING * around(basis[-1]))

    parts[0] = start[GHOST : GHOST + high, 0:wide]
    for i in range(ITERS):
        parts[1 + i] = basis[i][GHOST : GHOST + high, 0:wide]
    results[1] = start_buf[1, GHOST : GHOST + high, 0:wide]

    def store(i):
        return pltpu.make_async_copy(results.at[i], parts_out.at[i], store_sem.at[i])

    own = inside & (row_at >= 0) & (row_at < high) & (lane_at < wide)
    for m in range(2 * ITERS):
        product = jnp.where(own, basis[m // 2] * basis[m - m // 2], 0.0)
        line = jnp.sum(product, axis=0, keepdims=True)
        total = line[:, 0:LANES]
        for strip in range(1, wide // LANES):
            total = total + line[:, strip * LANES : (strip + 1) * LANES]
        mine[m : m + 1, :] = total
    mine[2 * ITERS :, :] = jnp.zeros((8 - 2 * ITERS, LANES), jnp.float32)

    def row_share(k):
        return pltpu.make_async_remote_copy(
            src_ref=mine,
            dst_ref=row_part.at[my_row],
            send_sem=rsum_ss.at[k],
            recv_sem=rsum_rs.at[my_row],
            device_id=(row_peer(k), my_col),
            device_id_type=MESH,
        )

    def row_arrival(k):
        who = row_peer(k)
        return pltpu.make_async_remote_copy(
            src_ref=mine,
            dst_ref=row_part.at[who],
            send_sem=rsum_ss.at[k],
            recv_sem=rsum_rs.at[who],
            device_id=(who, my_col),
            device_id_type=MESH,
        )

    for k in range(1, rows):
        row_share(k).start()
    store(1).start()
    row_part[my_row] = mine[...]
    for k in range(1, rows):
        row_arrival(k).wait_recv()
    strip_sum = row_part[0]
    for k in range(1, rows):
        strip_sum = strip_sum + row_part[k]
    col_part[my_col] = strip_sum

    def col_share(k, slot):
        return pltpu.make_async_remote_copy(
            src_ref=col_part.at[my_col],
            dst_ref=col_part.at[slot],
            send_sem=csum_ss.at[k],
            recv_sem=csum_rs.at[slot],
            device_id=(my_row, col_peer(k)),
            device_id_type=MESH,
        )

    for k in range(1, cols):
        col_share(k, my_col).start()
    for k in range(1, cols):
        col_share(k, col_peer(k)).wait_recv()
    everything = col_part[0]
    for k in range(1, cols):
        everything = everything + col_part[k]
    everything = jnp.sum(everything, axis=1, keepdims=True)
    moments = [everything[m : m + 1, :] for m in range(2 * ITERS)]
    answer = solve_coefficients(moments)
    result = parts[0]
    for i, scale in enumerate(answer):
        result = result + scale * parts[1 + i]
    results[0] = result
    store(0).start()

    for side in (0, 1):
        @pl.when(has[side])
        def _(side=side):
            for channel in range(CHANNELS):
                row_copy(side, channel).wait_send()
            corner_copy(side).wait_send()

        pl.when(beside[side])(lambda side=side: col_copy(side).wait_send())
    for k in range(1, rows):
        row_share(k).wait_send()
    for i in (0, 1):
        store(i).wait()
    for k in range(1, cols):
        col_share(k, my_col).wait_send()


def local(counts, scatter_vectors, ground_ratio, vertical_wavenumber, initial_phase, initial_extinction):
    high, wide = initial_phase.shape
    rows, cols = counts
    vectors = scatter_vectors.reshape(RAW, high, wide)
    full = wide + LANES
    tall = high + 2 * GHOST
    edges_at = [0]
    for channel in range(CHANNELS):
        held = 4 * REACH + (GUESS * GHOST if channel == 0 else 0)
        edges_at.append(edges_at[-1] + -(-held // 8) * 8)
    edge = edges_at[-1]
    packed = -(-(RAW + GUESS) * SLOT // LANES) * LANES
    f32 = jnp.float32
    dma = pltpu.SemaphoreType.DMA
    out = jax.ShapeDtypeStruct((2, high, wide), f32)
    results = pl.pallas_call(
        functools.partial(kernel, counts, edges_at),
        out_shape=out,
        in_specs=[pl.BlockSpec(memory_space=pltpu.HBM)] * 5,
        out_specs=pl.BlockSpec(memory_space=pltpu.HBM),
        scratch_shapes=[
            pltpu.SMEM((CHANNELS,), f32),
            pltpu.VMEM((RAW, high, wide), f32),
            pltpu.VMEM((high, wide), f32),
            pltpu.VMEM((high, wide), f32),
            pltpu.VMEM((high, wide), f32),
            dma((5,)),
            dma((2,)),
            pltpu.VMEM((2, high, wide), f32),
            pltpu.VMEM((3, tall, full), f32),
            pltpu.VMEM((1 + ITERS, high, wide), f32),
            pltpu.VMEM((5, tall, full), f32),
            pltpu.VMEM((2, edge, wide), f32),
            pltpu.VMEM((2, edge, wide), f32),
            pltpu.VMEM((2, high, packed), f32),
            pltpu.VMEM((2, high, packed), f32),
            pltpu.VMEM((2, 2, SLOT, packed), f32),
            pltpu.VMEM((GUESS, tall, full), f32),
            pltpu.VMEM((RAW, tall, full), f32),
            pltpu.VMEM((tall, full), f32),
            pltpu.VMEM((2, tall, full), f32),
            pltpu.VMEM((8, LANES), f32),
            pltpu.VMEM((rows, 8, LANES), f32),
            pltpu.VMEM((cols, 8, LANES), f32),
            dma((2, CHANNELS)), dma((2, CHANNELS)), dma((2,)), dma((2,)), dma((2,)), dma((2,)),
            dma((rows,)), dma((rows,)), dma((cols,)), dma((cols,)),
        ],
        compiler_params=pltpu.CompilerParams(
            collective_id=0, has_side_effects=True, vmem_limit_bytes=56 * 1024 * 1024
        ),
        cost_estimate=pl.CostEstimate(
            flops=2000 * high * wide, bytes_accessed=80 * high * wide, transcendentals=8 * high * wide
        ),
    )(ground_ratio, vectors, vertical_wavenumber, initial_phase, initial_extinction)
    return (results[0], results[1])


def solution(mesh):
    placed = (
        P(None, None, None, "row", "col"),
        P(),
        P("row", "col"),
        P("row", "col"),
        P("row", "col"),
    )
    counts = (mesh.shape["row"], mesh.shape["col"])
    return jax.shard_map(
        functools.partial(local, counts),
        mesh=mesh,
        in_specs=placed,
        out_specs=(P("row", "col"), P("row", "col")),
        check_vma=False,
    )
```
